32 devices in a mesh: row: 4 (over y, x), col: 8 (over z, core).
Axes of the slice: x: 2, y: 2, z: 4, core: 2. Of those that a mesh axis runs over, the one named last changes fastest.
Arguments:
- probe_block: bfloat16 [64, 32768], P(None, ('row', 'col'))
- prior_blocks: bfloat16 [4, 64, 32768], P(None, None, ('row', 'col'))
- self_relatedness: float32 [32768], P(('row', 'col')), may hold values from 0.5 to 2
- tile_values: bfloat16 [160, 1024, 1024], P(('row', 'col')), may hold values from -0.125 to 0.125
- tile_index: int32 [160, 3], P(('row', 'col')), may hold values from 0 to 31, as said below
Outputs:
- residual_block: float32 [64, 32768], P(None, ('row', 'col'))
- coefficients: float32 [5, 64, 64], replicated
The draws below stay inside these ranges and needn't reach their ends.
Inputs may be any that keep to these rules, and one draw needn't show every extreme that they name: `tile_index`: rows d * 5 to d * 5 + 4 belong to the device d = r * C + c at mesh position (r, c), C the size of the col axis. In a row with column 2 equal to 1 (live) the tile row lies in [r * C, r * C + C), the tile column j has j % C == c, and tile row <= tile column; live pairs of one device are distinct. Column 2 is 0 in dead rows, which repeat the indices of the device's first row. Live counts vary between devices (not all equal), and some device has all 5 rows live.
All inputs are finite; a program needn't handle non-finite values.
Results may differ from the reference program's by a relative error of at most 0.0003.
Values may be sent and summed in bfloat16 or wider, within the bound.
A program may use at most 128 MiB of HBM per device.

```python
import math
import jax
import jax.numpy as jnp
from jax import lax

K = 64
TS = 1024
BLOCKS = 4
SLOTS = 5
NQ = 5
NS = 32768
N_ROW = 4
N_COL = 8


def fresh_noise(key, shape):
    return jax.random.normal(key, shape, jnp.float32)


def shared_parts(key):
    scale_key = jax.random.fold_in(key, 31)
    shared_key = jax.random.fold_in(key, 32)
    position = jnp.arange(NS, dtype=jnp.float32)
    rising = jnp.sqrt(1.0 + 2.0 * position / NS)
    spread = jnp.exp(jax.random.uniform(scale_key, (NS,), jnp.float32, math.log(0.4), math.log(4.0)))
    common = 0.6 * jax.random.normal(shared_key, (K, NS), jnp.float32)
    return (common, spread * rising)


def draw_probe_block(key, part):
    common, scales = shared_parts(key)
    own = fresh_noise(jax.random.fold_in(key, 21), (K, NS))
    return ((own + common) * scales[None, :]).astype(jnp.bfloat16)


def draw_prior_blocks(key, part):
    common, scales = shared_parts(key)
    own = fresh_noise(jax.random.fold_in(key, 22), (BLOCKS, K, NS))
    return ((own + common[None]) * scales[None, None, :]).astype(jnp.bfloat16)


def draw_tile_index(key, part):
    devices = N_ROW * N_COL
    device = jnp.arange(devices, dtype=jnp.int32)[:, None]
    candidate = jnp.arange(devices, dtype=jnp.int32)[None, :]
    row_block = device // N_COL
    col_set = device % N_COL
    tile_row = row_block * N_COL + candidate // N_ROW
    tile_col = candidate % N_ROW * N_COL + col_set
    allowed = tile_row <= tile_col
    scores = jax.random.randint(jax.random.fold_in(key, 41), (devices, devices), 0, 1 << 20) * devices + candidate
    ranked = jnp.where(allowed, scores, (1 << 30) + candidate)
    order = jnp.argsort(ranked, axis=1)[:, :SLOTS]
    picked_row = jnp.take_along_axis(jnp.broadcast_to(tile_row, (devices, devices)), order, axis=1)
    picked_col = jnp.take_along_axis(jnp.broadcast_to(tile_col, (devices, devices)), order, axis=1)
    available = jnp.sum(allowed.astype(jnp.int32), axis=1)
    first_draw = jax.random.randint(jax.random.fold_in(key, 42), (devices,), 0, SLOTS)
    second_draw = jax.random.randint(jax.random.fold_in(key, 43), (devices,), 0, SLOTS)
    wanted = 1 + jnp.minimum(first_draw, second_draw)
    full_device = jax.random.randint(jax.random.fold_in(key, 44), (), 0, N_COL)
    wanted = jnp.where(jnp.arange(devices, dtype=jnp.int32) == full_device, SLOTS, wanted)
    active_count = jnp.minimum(wanted, available)
    slot_number = jnp.arange(SLOTS, dtype=jnp.int32)[None, :]
    active = slot_number < active_count[:, None]
    rows_out = jnp.where(active, picked_row, picked_row[:, :1])
    cols_out = jnp.where(active, picked_col, picked_col[:, :1])
    flags = active.astype(jnp.int32)
    table = jnp.stack([rows_out, cols_out, flags], axis=-1)
    return table.reshape(devices * SLOTS, 3).astype(jnp.int32)


def steps_of(key, shape, shards, smallest, high):
    level = 1.0
    for dim, blocks in shards:
        draws = jax.random.uniform(jax.random.fold_in(jax.random.fold_in(key, 6), dim), (blocks,), jnp.float32, smallest / len(shards), high / len(shards))
        level = level * jnp.repeat(jnp.exp(draws), shape[dim] // blocks).reshape((-1,) + (1,) * (len(shape) - 1 - dim))
    return level


def bell_draw(stream_key, extent, scale, most, shards=(), kind=jnp.bfloat16):
    entries = jax.random.normal(stream_key, extent, jnp.float32) * scale
    if len(shards) > 0:
        entries = steps_of(stream_key, extent, shards, -0.22, 0.18) * entries
    return jnp.clip(entries, min=-most, max=most).astype(kind)


def setup_inputs(seed: int = 0) -> dict:
    key_of = jax.random.split(jax.random.key(seed), 6)
    return {
        "probe_block": draw_probe_block(jax.random.fold_in(key_of[5], 71), 0),
        "prior_blocks": draw_prior_blocks(jax.random.fold_in(key_of[5], 71), 0),
        "self_relatedness": jnp.clip(jnp.exp(math.log(2.0) - 1.3862944 * jax.random.uniform(key_of[2], (NS,), jnp.float32) ** steps_of(key_of[2], (NS,), ((0, 32),), -0.2, 0.2)), 0.5, 2.0),
        "tile_values": bell_draw(key_of[3], (N_ROW * N_COL * SLOTS, TS, TS), (2 * TS) ** -0.5, 0.125, ((0, 32),)),
        "tile_index": draw_tile_index(jax.random.fold_in(key_of[5], 71), 0),
    }


def add_span(running, addend, offset):
    current = lax.dynamic_slice_in_dim(running, offset, addend.shape[1], 1)
    return lax.dynamic_update_slice_in_dim(running, current + addend, offset, 1)

def keep_same(running):
    return running

def reference(probe_block, prior_blocks, self_relatedness, tile_values, tile_index):
    tile_width = tile_values.shape[1]
    start = self_relatedness[None, :] * probe_block.astype(jnp.float32)

    def accumulate(running, inputs):
        current_tile, entry = inputs

        def apply(state):
            row_start = (entry[0] * tile_width).astype(jnp.int32)
            col_start = (entry[1] * tile_width).astype(jnp.int32)
            right = lax.dynamic_slice_in_dim(probe_block, col_start, tile_width, 1)
            left = lax.dynamic_slice_in_dim(probe_block, row_start, tile_width, 1)
            forward = lax.dot_general(right.astype(jnp.float32), current_tile.astype(jnp.float32), (((1,), (1,)), ((), ())), preferred_element_type=jnp.float32)
            mirror = jnp.dot(left.astype(jnp.float32), current_tile.astype(jnp.float32), preferred_element_type=jnp.float32)
            state = add_span(state, forward, row_start)
            return add_span(state, mirror, col_start)
        return (lax.cond(entry[2] > 0, apply, keep_same, running), None)
    product, _ = lax.scan(accumulate, start, (tile_values, tile_index))
    basis = jnp.concatenate([prior_blocks, probe_block[None]], axis=0)
    current = product
    solved = []
    for block_number in range(NQ):
        basis_block = basis[block_number]
        gram_block = jnp.dot(basis_block.astype(jnp.float32), basis_block.T.astype(jnp.float32), preferred_element_type=jnp.float32)
        wide_block = basis_block.astype(jnp.float32)
        along = jnp.dot(wide_block, current.T, precision=lax.Precision.HIGHEST)
        factor = jnp.linalg.cholesky(gram_block)
        coefficient = jax.scipy.linalg.cho_solve((factor, True), along)
        solved.append(coefficient)
        current = current - jnp.dot(coefficient.T, wide_block, precision=lax.Precision.HIGHEST)
    return (current, jnp.stack(solved))
```

```python
import jax
import jax.numpy as jnp
from jax import lax
from jax.sharding import PartitionSpec as P

HIGH = lax.Precision.HIGHEST


def add_span(running, addend, offset):
    current = lax.dynamic_slice_in_dim(running, offset, addend.shape[1], 1)
    return lax.dynamic_update_slice_in_dim(running, current + addend, offset, 1)


def keep_same(partials):
    return partials


def tile_products(tile_values, tile_index, row_probes, col_probes, col_count):
    tile_width = tile_values.shape[1]
    depth = row_probes.shape[0]
    partials = (
        jnp.zeros((depth, row_probes.shape[1]), jnp.float32),
        jnp.zeros((depth, col_probes.shape[1]), jnp.float32),
    )
    for slot_index in range(tile_values.shape[0]):
        current_tile = tile_values[slot_index]
        row_start = tile_index[slot_index, 0] % col_count * tile_width
        col_start = tile_index[slot_index, 1] // col_count * tile_width

        def apply(state, current_tile=current_tile, row_start=row_start, col_start=col_start):
            right = lax.dynamic_slice_in_dim(col_probes, col_start, tile_width, 1)
            forward = lax.dot_general(
                right, current_tile, (((1,), (1,)), ((), ())), preferred_element_type=jnp.float32
            )
            left = lax.dynamic_slice_in_dim(row_probes, row_start, tile_width, 1)
            mirror = jnp.dot(left, current_tile, preferred_element_type=jnp.float32)
            return (add_span(state[0], forward, row_start), add_span(state[1], mirror, col_start))

        partials = lax.cond(tile_index[slot_index, 2] > 0, apply, keep_same, partials)
    return partials


def shards(probe_block, prior_blocks, self_relatedness, tile_values, tile_index):
    col_count = lax.axis_size("col")
    blocks = prior_blocks.shape[0] + 1
    depth = probe_block.shape[0]
    basis = jnp.concatenate([prior_blocks, probe_block[None]], axis=0).reshape(blocks * depth, -1)
    gram = lax.psum(jnp.dot(basis, basis.T, preferred_element_type=jnp.float32), ("row", "col"))
    gram = gram.reshape(blocks, depth, blocks, depth)
    diagonal = jnp.stack([gram[b, :, b] for b in range(blocks)])
    eye = jnp.broadcast_to(jnp.eye(depth, dtype=jnp.float32), diagonal.shape)
    inverse = jax.scipy.linalg.cho_solve((jnp.linalg.cholesky(diagonal), True), eye)
    row_probes = lax.all_gather(probe_block, "col", axis=1, tiled=True)
    col_probes = lax.all_gather(probe_block, "row", axis=1, tiled=True)
    row_part, col_part = tile_products(tile_values, tile_index, row_probes, col_probes, col_count)
    row_total = lax.psum_scatter(row_part, "col", scatter_dimension=1, tiled=True)
    col_total = lax.psum_scatter(col_part, "row", scatter_dimension=1, tiled=True)
    product = self_relatedness[None, :] * probe_block.astype(jnp.float32) + row_total + col_total
    wide = basis.astype(jnp.float32)
    along = lax.psum(jnp.dot(wide, product.T, precision=HIGH), ("row", "col")).reshape(blocks, depth, depth)
    solved = []
    for b in range(blocks):
        target = along[b]
        for a in range(b):
            target = target - jnp.dot(gram[b, :, a], solved[a], precision=HIGH)
        solved.append(jnp.dot(inverse[b], target, precision=HIGH))
    stacked = jnp.stack(solved)
    current = product - jnp.dot(stacked.reshape(blocks * depth, depth).T, wide, precision=HIGH)
    return (current, stacked)


def solution(mesh):
    in_specs = (
        P(None, ("row", "col")),
        P(None, None, ("row", "col")),
        P(("row", "col")),
        P(("row", "col"), None, None),
        P(("row", "col"), None),
    )
    out_specs = (P(None, ("row", "col")), P())
    return jax.shard_map(shards, mesh=mesh, in_specs=in_specs, out_specs=out_specs, check_vma=False)
```

```python
import functools

import jax
import jax.numpy as jnp
from jax import lax
from jax.experimental import pallas as pl
from jax.experimental.pallas import tpu as pltpu
from jax.sharding import PartitionSpec as P

HIGH = lax.Precision.HIGHEST
MESH = pl.DeviceIdType.MESH
F32 = jnp.float32
BF16 = jnp.bfloat16
NT = (((1,), (1,)), ((), ()))
TN = (((0,), (0,)), ((), ()))


def round_up(value, unit):
    return -(-value // unit) * unit


def split3(x):
    hi = x.astype(BF16)
    rest = x - hi.astype(F32)
    mid = rest.astype(BF16)
    lo = (rest - mid.astype(F32)).astype(BF16)
    return hi, mid, lo


def lane_of(shape):
    return lax.broadcasted_iota(jnp.int32, shape, len(shape) - 1)


def pack(block):
    half = block.shape[0] // 2
    return jnp.where(lane_of((half, block.shape[1])) < block.shape[1] // 2, block[:half], block[half:])


def unpack(packed):
    width = packed.shape[1] // 2
    return jnp.concatenate([packed[:, :width], pltpu.roll(packed, width, 1)[:, :width]], axis=0)


def kernel(
    R, C, S, B, K, g_rows, h_rows,
    index_ref, probe_ref, prior_ref, self_ref, tiles_ref,
    out_ref, coef_ref,
    tile_buf, basis, rowp, colp, fwd, mir, row_part, sib_in, z_send, z_in, col_part, col_in,
    g_buf, g1, g2, g2_in, g3, g4, h_buf, h1, h2, h2_in, h3, h4, aug, mult,
    tile_sem, gz_s, gz_r, gs_s, gs_r, gr_s, gr_r, sb_s, sb_r, zz_s, zz_r, cc_s, cc_r, red_row_s, red_row_r, red_col_s, red_col_r,
):
    Z = C // 2
    r, c = lax.axis_index("row"), lax.axis_index("col")
    z, core = c // 2, c % 2
    sib = z * 2 + (1 - core)
    pairs = [(b, a) for a in range(B) for b in range(a, B)]

    def local(s):
        return pltpu.make_async_copy(tiles_ref.at[s], tile_buf.at[s], tile_sem.at[s])

    def remote(src, dst, ssem, rsem, row, col):
        return pltpu.make_async_remote_copy(
            src_ref=src, dst_ref=dst, send_sem=ssem, recv_sem=rsem, device_id=(row, col), device_id_type=MESH
        )

    def loop(n, body):
        def step(k, carry):
            body(k)
            return carry

        lax.fori_loop(0, n, step, 0)

    loop(S, lambda s: local(s).start())

    barrier = pltpu.get_barrier_semaphore()
    loop(C - 1, lambda k: pl.semaphore_signal(barrier, inc=1, device_id=(r, (c + 1 + k) % C), device_id_type=MESH))
    loop(R - 1, lambda k: pl.semaphore_signal(barrier, inc=1, device_id=((r + 1 + k) % R, c), device_id_type=MESH))
    pl.semaphore_wait(barrier, C + R - 2)

    def row_gather(k):
        peer = (r + 1 + k) % R
        return remote(probe_ref, colp.at[r], gr_s.at[peer], gr_r.at[r], peer, c)

    def z_gather(k):
        peer = (z + 1 + k) % Z
        return remote(probe_ref, rowp.at[c], gz_s.at[peer], gz_r.at[z], r, peer * 2 + core)

    def sib_gather(zz):
        slot = zz * 2 + core
        return remote(rowp.at[slot], rowp.at[slot], gs_s.at[zz], gs_r.at[zz], r, sib)

    def sib_arrival(zz):
        slot = zz * 2 + (1 - core)
        return remote(rowp.at[slot], rowp.at[slot], gs_s.at[zz], gs_r.at[zz], r, sib)

    loop(R - 1, lambda k: row_gather(k).start())
    loop(Z - 1, lambda k: z_gather(k).start())
    rowp[c] = probe_ref[...]
    colp[r] = probe_ref[...]
    sib_gather(z).start()

    def reducer(which, buf, in1, buf2, in2, all3, all4, rows):
        chunk = C * rows

        def p1(k):
            peer = (r + 1 + k) % R
            src = buf.at[pl.ds(pl.multiple_of(peer * chunk, 8), chunk)]
            return remote(src, in1.at[r], red_row_s.at[which, 0, peer], red_row_r.at[which, 0, r], peer, c)

        def p2(k):
            peer = (c + 1 + k) % C
            src = buf2.at[pl.ds(pl.multiple_of(peer * rows, 8), rows)]
            return remote(src, in2.at[c], red_col_s.at[which, 0, peer], red_col_r.at[which, 0, c], r, peer)

        def p3(k):
            peer = (c + 1 + k) % C
            return remote(all3.at[c], all3.at[c], red_col_s.at[which, 1, peer], red_col_r.at[which, 1, c], r, peer)

        def p4(k):
            peer = (r + 1 + k) % R
            return remote(all3, all4.at[r], red_row_s.at[which, 1, peer], red_row_r.at[which, 1, r], peer, c)

        def got_row(phase, dst, k):
            peer = (r + 1 + k) % R
            remote(dst.at[peer], dst.at[peer], red_row_s.at[which, phase, peer], red_row_r.at[which, phase, peer], peer, c).wait_recv()

        def got_col(phase, dst, k):
            peer = (c + 1 + k) % C
            remote(dst.at[peer], dst.at[peer], red_col_s.at[which, phase, peer], red_col_r.at[which, phase, peer], r, peer).wait_recv()

        def first():
            loop(R - 1, lambda k: p1(k).start())

        def second():
            buf2[...] = buf[pl.ds(pl.multiple_of(r * chunk, 8), chunk), :]

            def add(k):
                got_row(0, in1, k)
                buf2[...] += in1[(r + 1 + k) % R]

            loop(R - 1, add)
            loop(C - 1, lambda k: p2(k).start())

        def third():
            def add(k, total):
                got_col(0, in2, k)
                return total + in2[(c + 1 + k) % C]

            all3[c] = lax.fori_loop(0, C - 1, add, buf2[pl.ds(pl.multiple_of(c * rows, 8), rows), :])
            loop(C - 1, lambda k: p3(k).start())

        def fourth():
            loop(C - 1, lambda k: got_col(1, all3, k))
            loop(R - 1, lambda k: p4(k).start())
            all4[r] = all3[...]

        def fifth():
            loop(R - 1, lambda k: got_row(1, all4, k))

        def drain():
            loop(R - 1, lambda k: p1(k).wait_send())
            loop(C - 1, lambda k: p2(k).wait_send())
            loop(C - 1, lambda k: p3(k).wait_send())
            loop(R - 1, lambda k: p4(k).wait_send())

        return first, second, third, fourth, fifth, drain

    gram = reducer(0, g_buf, g1, g2, g2_in, g3, g4, g_rows)
    along = reducer(1, h_buf, h1, h2, h2_in, h3, h4, h_rows)

    for b in range(B - 1):
        basis[b * K : (b + 1) * K, :] = prior_ref[b]
    basis[(B - 1) * K :, :] = probe_ref[...]
    half = K // 2
    used = len(pairs) * half
    spot = 0
    for a in range(B):
        one = basis[a * K : (a + 1) * K, :]
        both = jnp.concatenate([one, one], axis=0)
        blocks = lax.dot_general(basis[a * K :, :], both, NT, preferred_element_type=F32)
        for b in range(a, B):
            g_buf[spot : spot + half, :] = pack(blocks[(b - a) * K : (b - a + 1) * K])
            spot += half
    if g_buf.shape[0] > used:
        g_buf[used:, :] = jnp.zeros((g_buf.shape[0] - used, 2 * K), F32)
    if h_buf.shape[0] > B * half:
        h_buf[B * half :, :] = jnp.zeros((h_buf.shape[0] - B * half, 2 * K), F32)
    gram[0]()

    def got_row_probe(k):
        peer = (r + 1 + k) % R
        remote(colp.at[peer], colp.at[peer], gr_s.at[peer], gr_r.at[peer], peer, c).wait_recv()

    loop(R - 1, got_row_probe)

    def forward(s):
        local(s).wait()
        right = colp[index_ref[s, 1] // C]
        fwd[s] = lax.dot_general(right, tile_buf[s], NT, preferred_element_type=F32)

    loop(S, forward)

    def share_probe(k):
        peer = (z + 1 + k) % Z
        slot = peer * 2 + core
        remote(rowp.at[slot], rowp.at[slot], gz_s.at[peer], gz_r.at[peer], r, slot).wait_recv()
        sib_gather(peer).start()

    loop(Z - 1, share_probe)
    gram[1]()

    def pick(parts, column, number, modulus, divide):
        def add(s, total):
            value = index_ref[s, column]
            place = value // C if divide else value % C
            hit = jnp.logical_and(place == number, index_ref[s, 2] > 0)
            return total + jnp.where(hit, parts[s], 0.0)

        return lax.fori_loop(0, S, add, jnp.zeros(parts.shape[1:], F32))

    def to_sib(zz):
        return remote(row_part.at[zz], sib_in.at[zz], sb_s.at[zz], sb_r.at[zz], r, sib)

    def give_sib(k):
        zz = (z + 1 + k) % Z
        row_part[zz] = pick(fwd, 0, zz * 2 + (1 - core), C, False)
        to_sib(zz).start()

    loop(Z, give_sib)

    def to_z(zz):
        return remote(z_send.at[zz], z_in.at[z], zz_s.at[zz], zz_r.at[z], r, zz * 2 + core)

    def chip_sum(zz):
        mine = pick(fwd, 0, zz * 2 + core, C, False)
        to_sib(zz).wait_recv()
        z_send[zz] = mine + sib_in[zz]

    def give_z(k):
        zz = (z + 1 + k) % Z
        chip_sum(zz)
        to_z(zz).start()

    loop(Z - 1, give_z)

    loop(Z, lambda zz: sib_arrival(zz).wait_recv())

    def mirror(s):
        left = rowp[index_ref[s, 0] % C]
        mir[s] = jnp.dot(left, tile_buf[s], preferred_element_type=F32)

    loop(S, mirror)

    def to_row(peer):
        return remote(col_part.at[peer], col_in.at[r], cc_s.at[peer], cc_r.at[r], peer, c)

    def give_row(k):
        peer = (r + 1 + k) % R
        col_part[peer] = pick(mir, 1, peer, C, True)
        to_row(peer).start()

    loop(R - 1, give_row)
    gram[2]()
    chip_sum(z)
    out_ref[...] = (
        self_ref[...] * probe_ref[...].astype(F32) + z_send[z] + pick(mir, 1, r, C, True)
    )
    gram[3]()
    gram[4]()

    sums = g4[...].reshape(-1, 2 * K)
    gram_blocks = {}
    lanes = lane_of((K, 2 * K))
    down = lax.broadcasted_iota(jnp.int32, (K, 2 * K), 0)
    eye = jnp.where(lanes == down + K, 1.0, 0.0)
    for i, (b, a) in enumerate(pairs):
        packed = sums[i * half : (i + 1) * half]
        if a == b:
            whole = jnp.concatenate([packed, pltpu.roll(packed, K, 1)], axis=0)
            aug[b] = jnp.where(lanes < K, whole, eye)
        else:
            gram_blocks[b, a] = unpack(packed)

    all_lanes = lane_of((B, K, 2 * K))
    all_down = lax.broadcasted_iota(jnp.int32, (B, K, 2 * K), 1)
    row_lanes = lane_of((B, 1, 2 * K))

    def eliminate(k):
        whole = aug[...]
        row = aug[:, pl.ds(k, 1), :]
        column = jnp.sum(jnp.where(all_lanes == k, whole, 0.0), axis=2, keepdims=True)
        pivot = jnp.sum(jnp.where(row_lanes == k, row, 0.0), axis=2, keepdims=True)
        scaled = row / pivot
        aug[...] = jnp.where(all_down == k, scaled, whole - column * scaled)

    loop(K, eliminate)
    inverse = [pltpu.roll(aug[b], K, 1)[:, :K] for b in range(B)]
    for i, (b, a) in enumerate(pairs):
        if a != b:
            mult[i] = jnp.dot(inverse[b], gram_blocks[b, a], precision=HIGH, preferred_element_type=F32)

    def add_row(k):
        peer = (r + 1 + k) % R
        remote(col_in.at[peer], col_in.at[peer], cc_s.at[peer], cc_r.at[peer], peer, c).wait_recv()
        out_ref[...] += col_in[peer]

    loop(R - 1, add_row)

    def add_z(k):
        peer = (z + 1 + k) % Z
        remote(z_in.at[peer], z_in.at[peer], zz_s.at[peer], zz_r.at[peer], r, peer * 2 + core).wait_recv()
        out_ref[...] += z_in[peer]

    loop(Z - 1, add_z)

    product = out_ref[...]
    inner = jnp.zeros((B * K, 2 * K), F32)
    for part in split3(product)[::-1]:
        both = jnp.concatenate([part, part], axis=0)
        inner = inner + lax.dot_general(basis[...], both, NT, preferred_element_type=F32)
    for b in range(B):
        h_buf[b * half : (b + 1) * half, :] = pack(inner[b * K : (b + 1) * K])
    for phase in along[:5]:
        phase()
    targets = h4[...].reshape(-1, 2 * K)
    solved = []
    for b in range(B):
        target = unpack(targets[b * half : (b + 1) * half])
        value = jnp.dot(inverse[b], target, precision=HIGH, preferred_element_type=F32)
        for a in range(b):
            value = value - jnp.dot(mult[pairs.index((b, a))], solved[a], precision=HIGH, preferred_element_type=F32)
        solved.append(value)
        coef_ref[b] = value
    stacked = jnp.concatenate(solved, axis=0)
    taken = jnp.zeros(product.shape, F32)
    for part in split3(stacked.T)[::-1]:
        taken = taken + jnp.dot(part, basis[...], preferred_element_type=F32)
    out_ref[...] = product - taken

    gram[5]()
    along[5]()
    loop(R - 1, lambda k: row_gather(k).wait_send())
    loop(Z - 1, lambda k: z_gather(k).wait_send())
    loop(Z, lambda zz: sib_gather(zz).wait_send())
    loop(Z, lambda zz: to_sib(zz).wait_send())
    loop(Z - 1, lambda k: to_z((z + 1 + k) % Z).wait_send())
    loop(R - 1, lambda k: to_row((r + 1 + k) % R).wait_send())


def shards(R, C, probe_block, prior_blocks, self_relatedness, tile_values, tile_index):
    K, T = probe_block.shape
    S = tile_values.shape[0]
    B = prior_blocks.shape[0] + 1
    Z = C // 2
    half = K // 2
    g_rows = round_up(-(-(B * (B + 1) // 2 * half) // (R * C)), 8)
    h_rows = round_up(-(-(B * half) // (R * C)), 8)
    vmem = lambda shape, dtype=F32: pltpu.VMEM(shape, dtype)
    dma = lambda *shape: pltpu.SemaphoreType.DMA(shape)
    W = 2 * K

    def reduce_scratch(rows):
        return [
            vmem((R * C * rows, W)), vmem((R, C * rows, W)), vmem((C * rows, W)),
            vmem((C, rows, W)), vmem((C, rows, W)), vmem((R, C, rows, W)),
        ]

    scratch = [
        vmem((S, T, T), BF16), vmem((B * K, T), BF16), vmem((C, K, T), BF16), vmem((R, K, T), BF16),
        vmem((S, K, T)), vmem((S, K, T)),
        vmem((Z, K, T)), vmem((Z, K, T)), vmem((Z, K, T)), vmem((Z, K, T)),
        vmem((R, K, T)), vmem((R, K, T)),
        *reduce_scratch(g_rows), *reduce_scratch(h_rows),
        vmem((B, K, W)), vmem((B * (B + 1) // 2, K, K)),
        dma(S), dma(Z), dma(Z), dma(Z), dma(Z), dma(R), dma(R), dma(Z), dma(Z), dma(Z), dma(Z), dma(R), dma(R),
        dma(2, 2, R), dma(2, 2, R), dma(2, 2, C), dma(2, 2, C),
    ]
    in_vmem = pl.BlockSpec(memory_space=pltpu.VMEM)
    residual, coefficients = pl.pallas_call(
        functools.partial(kernel, R, C, S, B, K, g_rows, h_rows),
        out_shape=(jax.ShapeDtypeStruct((K, T), F32), jax.ShapeDtypeStruct((B, K, K), F32)),
        in_specs=[
            pl.BlockSpec(memory_space=pltpu.SMEM), in_vmem, in_vmem, in_vmem, pl.BlockSpec(memory_space=pl.ANY),
        ],
        out_specs=(in_vmem, in_vmem),
        scratch_shapes=scratch,
        compiler_params=pltpu.CompilerParams(
            collective_id=0, has_side_effects=True, vmem_limit_bytes=56 * 1024 * 1024
        ),
        cost_estimate=pl.CostEstimate(
            flops=4 * S * K * T * T, bytes_accessed=2 * S * T * T, transcendentals=0
        ),
    )(tile_index, probe_block, prior_blocks, self_relatedness[None], tile_values)
    return (residual, coefficients)


def solution(mesh):
    in_specs = (
        P(None, ("row", "col")),
        P(None, None, ("row", "col")),
        P(("row", "col")),
        P(("row", "col"), None, None),
        P(("row", "col"), None),
    )
    out_specs = (P(None, ("row", "col")), P())
    body = functools.partial(shards, mesh.shape["row"], mesh.shape["col"])
    return jax.shard_map(body, mesh=mesh, in_specs=in_specs, out_specs=out_specs, check_vma=False)
```

```python
import functools

import jax
import jax.numpy as jnp
from jax import lax
from jax.experimental import pallas as pl
from jax.experimental.pallas import tpu as pltpu
from jax.sharding import PartitionSpec as P

HIGH = lax.Precision.HIGHEST
MESH = pl.DeviceIdType.MESH
F32 = jnp.float32
BF16 = jnp.bfloat16
I16 = jnp.int16
NT = (((1,), (1,)), ((), ()))


def round_up(value, unit):
    return -(-value // unit) * unit


def split3(x):
    hi = x.astype(BF16)
    rest = x - hi.astype(F32)
    mid = rest.astype(BF16)
    lo = (rest - mid.astype(F32)).astype(BF16)
    return hi, mid, lo


def lane_of(shape):
    return lax.broadcasted_iota(jnp.int32, shape, len(shape) - 1)


def pack(block):
    half = block.shape[0] // 2
    return jnp.where(lane_of((half, block.shape[1])) < block.shape[1] // 2, block[:half], block[half:])


def unpack(packed):
    width = packed.shape[1] // 2
    return jnp.concatenate([packed[:, :width], pltpu.roll(packed, width, 1)[:, :width]], axis=0)


def code(block):
    rows = block.shape[0]
    most = jnp.maximum(jnp.max(jnp.abs(block), axis=1, keepdims=True), 1e-30)
    quantized = jnp.round(block * (32767.0 / most)).astype(jnp.int32).astype(jnp.int16)
    shape = (rows, 128)
    hit = lane_of(shape) == lax.broadcasted_iota(jnp.int32, shape, 0)
    line = jnp.sum(jnp.where(hit, most * (1.0 / 32767.0), 0.0), axis=0, keepdims=True)
    return quantized, jnp.broadcast_to(line, (8, 128))


def decode(quantized, lines):
    shape = (quantized.shape[0], 128)
    hit = lane_of(shape) == lax.broadcasted_iota(jnp.int32, shape, 0)
    scale = jnp.sum(jnp.where(hit, lines[:1], 0.0), axis=1, keepdims=True)
    return quantized.astype(jnp.int32).astype(F32) * scale


def kernel(
    R, C, S, B, K, g_rows, h_rows,
    index_in, probe_ref, prior_ref, self_ref, tiles_ref,
    out_ref, coef_ref,
    index_ref, tile_buf, basis, rowp, colp, fwd, mir, row_part, sib_in, z_sum, z_send, z_in, z_send_scale, z_in_scale,
    col_send, col_in, col_send_scale, col_in_scale,
    g_buf, g1, g2, g2_in, g3, g4, h_buf, h1, h2, h3, aug, solver,
    index_sem, tile_sem, gz_s, gz_r, gs_s, gs_r, gr_s, gr_r, sb_s, sb_r, zz_s, zz_r, zs_s, zs_r, cc_s, cc_r, cs_s, cs_r,
    red_row_s, red_row_r, red_col_s, red_col_r, al_row_s, al_row_r, al_col_s, al_col_r,
):
    Z = C // 2
    r, c = lax.axis_index("row"), lax.axis_index("col")
    z, core = c // 2, c % 2
    sib = z * 2 + (1 - core)
    pairs = [(b, a) for a in range(B) for b in range(a, B)]

    def local(s):
        return pltpu.make_async_copy(tiles_ref.at[s], tile_buf.at[s], tile_sem.at[s])

    def remote(src, dst, ssem, rsem, row, col):
        return pltpu.make_async_remote_copy(
            src_ref=src, dst_ref=dst, send_sem=ssem, recv_sem=rsem, device_id=(row, col), device_id_type=MESH
        )

    def loop(n, body):
        def step(k, carry):
            body(k)
            return carry

        lax.fori_loop(0, n, step, 0)

    index_copy = pltpu.make_async_copy(index_in, index_ref, index_sem)
    index_copy.start()
    loop(S, lambda s: local(s).start())

    barrier = pltpu.get_barrier_semaphore()
    loop(C - 1, lambda k: pl.semaphore_signal(barrier, inc=1, device_id=(r, (c + 1 + k) % C), device_id_type=MESH))
    loop(R - 1, lambda k: pl.semaphore_signal(barrier, inc=1, device_id=((r + 1 + k) % R, c), device_id_type=MESH))
    pl.semaphore_wait(barrier, C + R - 2)

    def row_gather(k):
        peer = (r + 1 + k) % R
        return remote(probe_ref, colp.at[r], gr_s.at[peer], gr_r.at[r], peer, c)

    def z_gather(k):
        peer = (z + 1 + k) % Z
        return remote(probe_ref, rowp.at[c], gz_s.at[peer], gz_r.at[z], r, peer * 2 + core)

    def sib_gather(zz):
        slot = zz * 2 + core
        return remote(rowp.at[slot], rowp.at[slot], gs_s.at[zz], gs_r.at[zz], r, sib)

    def sib_arrival(zz):
        slot = zz * 2 + (1 - core)
        return remote(rowp.at[slot], rowp.at[slot], gs_s.at[zz], gs_r.at[zz], r, sib)

    loop(R - 1, lambda k: row_gather(k).start())
    loop(Z - 1, lambda k: z_gather(k).start())
    rowp[c] = probe_ref[...]
    colp[r] = probe_ref[...]
    sib_gather(z).start()

    def reducer(buf, in1, buf2, in2, all3, all4, rows):
        chunk = C * rows

        def p1(k):
            peer = (r + 1 + k) % R
            src = buf.at[pl.ds(pl.multiple_of(peer * chunk, 8), chunk)]
            return remote(src, in1.at[r], red_row_s.at[0, peer], red_row_r.at[0, r], peer, c)

        def p2(k):
            peer = (c + 1 + k) % C
            src = buf2.at[pl.ds(pl.multiple_of(peer * rows, 8), rows)]
            return remote(src, in2.at[c], red_col_s.at[0, peer], red_col_r.at[0, c], r, peer)

        def p3(k):
            peer = (c + 1 + k) % C
            return remote(all3.at[c], all3.at[c], red_col_s.at[1, peer], red_col_r.at[1, c], r, peer)

        def p4(k):
            peer = (r + 1 + k) % R
            return remote(all3, all4.at[r], red_row_s.at[1, peer], red_row_r.at[1, r], peer, c)

        def got_row(phase, dst, k):
            peer = (r + 1 + k) % R
            remote(dst.at[peer], dst.at[peer], red_row_s.at[phase, peer], red_row_r.at[phase, peer], peer, c).wait_recv()

        def got_col(phase, dst, k):
            peer = (c + 1 + k) % C
            remote(dst.at[peer], dst.at[peer], red_col_s.at[phase, peer], red_col_r.at[phase, peer], r, peer).wait_recv()

        def first():
            loop(R - 1, lambda k: p1(k).start())

        def second():
            buf2[...] = buf[pl.ds(pl.multiple_of(r * chunk, 8), chunk), :]

            def add(k):
                got_row(0, in1, k)
                buf2[...] += in1[(r + 1 + k) % R]

            loop(R - 1, add)
            loop(C - 1, lambda k: p2(k).start())

        def third():
            def add(k, total):
                got_col(0, in2, k)
                return total + in2[(c + 1 + k) % C]

            all3[c] = lax.fori_loop(0, C - 1, add, buf2[pl.ds(pl.multiple_of(c * rows, 8), rows), :])
            loop(C - 1, lambda k: p3(k).start())

        def fourth():
            loop(C - 1, lambda k: got_col(1, all3, k))
            loop(R - 1, lambda k: p4(k).start())
            all4[r] = all3[...]

        def fifth():
            loop(R - 1, lambda k: got_row(1, all4, k))

        def drain():
            loop(R - 1, lambda k: p1(k).wait_send())
            loop(C - 1, lambda k: p2(k).wait_send())
            loop(C - 1, lambda k: p3(k).wait_send())
            loop(R - 1, lambda k: p4(k).wait_send())

        return first, second, third, fourth, fifth, drain

    gram = reducer(g_buf, g1, g2, g2_in, g3, g4, g_rows)

    def a1(k):
        peer = (c + 1 + k) % C
        src = h_buf.at[pl.ds(pl.multiple_of(peer * h_rows, 8), h_rows)]
        return remote(src, h1.at[c], al_col_s.at[0, peer], al_col_r.at[0, c], r, peer)

    def a2(k):
        peer = (r + 1 + k) % R
        return remote(h2.at[r], h2.at[r], al_row_s.at[peer], al_row_r.at[r], peer, c)

    def a3(k):
        peer = (c + 1 + k) % C
        return remote(h3.at[c], h3.at[c], al_col_s.at[1, peer], al_col_r.at[1, c], r, peer)

    def got_a_col(phase, dst, k):
        peer = (c + 1 + k) % C
        remote(dst.at[peer], dst.at[peer], al_col_s.at[phase, peer], al_col_r.at[phase, peer], r, peer).wait_recv()

    def got_a_row(k):
        peer = (r + 1 + k) % R
        remote(h2.at[peer], h2.at[peer], al_row_s.at[peer], al_row_r.at[peer], peer, c).wait_recv()

    def reduce_along():
        loop(C - 1, lambda k: a1(k).start())

        def add(k, total):
            got_a_col(0, h1, k)
            return total + h1[(c + 1 + k) % C]

        h2[r] = lax.fori_loop(0, C - 1, add, h_buf[pl.ds(pl.multiple_of(c * h_rows, 8), h_rows), :])
        loop(R - 1, lambda k: a2(k).start())
        loop(R - 1, got_a_row)
        h3[c] = lax.fori_loop(1, R, lambda k, total: total + h2[k], h2[0])
        loop(C - 1, lambda k: a3(k).start())
        loop(C - 1, lambda k: got_a_col(1, h3, k))

    for b in range(B - 1):
        basis[b * K : (b + 1) * K, :] = prior_ref[b]
    basis[(B - 1) * K :, :] = probe_ref[...]
    half = K // 2
    used = len(pairs) * half
    spot = 0
    for a in range(B):
        one = basis[a * K : (a + 1) * K, :]
        both = jnp.concatenate([one, one], axis=0)
        blocks = lax.dot_general(basis[a * K :, :], both, NT, preferred_element_type=F32)
        for b in range(a, B):
            g_buf[spot : spot + half, :] = pack(blocks[(b - a) * K : (b - a + 1) * K])
            spot += half
    if g_buf.shape[0] > used:
        g_buf[used:, :] = jnp.zeros((g_buf.shape[0] - used, 2 * K), F32)
    if h_buf.shape[0] > B * half:
        h_buf[B * half :, :] = jnp.zeros((h_buf.shape[0] - B * half, 2 * K), F32)
    gram[0]()

    def got_row_probe(k):
        peer = (r + 1 + k) % R
        remote(colp.at[peer], colp.at[peer], gr_s.at[peer], gr_r.at[peer], peer, c).wait_recv()

    loop(R - 1, got_row_probe)
    index_copy.wait()

    def forward(s):
        local(s).wait()
        right = colp[index_ref[s, 1] // C]
        fwd[s] = lax.dot_general(tile_buf[s], right, NT, preferred_element_type=F32).T

    loop(S, forward)

    def share_probe(k):
        peer = (z + 1 + k) % Z
        slot = peer * 2 + core
        remote(rowp.at[slot], rowp.at[slot], gz_s.at[peer], gz_r.at[peer], r, slot).wait_recv()
        sib_gather(peer).start()

    loop(Z - 1, share_probe)
    gram[1]()

    def pick(dst, parts, column, number, divide):
        hits = []
        for slot in range(S):
            value = index_ref[slot, column]
            place = value // C if divide else value % C
            hits.append(jnp.logical_and(place == number, index_ref[slot, 2] > 0))

        def some(k):
            rows = pl.ds(pl.multiple_of(k * 16, 16), 16)
            total = jnp.where(hits[0], parts[0, rows, :], 0.0)
            for slot in range(1, S):
                total = total + jnp.where(hits[slot], parts[slot, rows, :], 0.0)
            dst[rows, :] = total

        loop(K // 16, some)

    def to_sib(zz):
        return remote(row_part.at[zz], sib_in.at[zz], sb_s.at[zz], sb_r.at[zz], r, sib)

    def give_sib(k):
        zz = (z + 1 + k) % Z
        pick(row_part.at[zz], fwd, 0, zz * 2 + (1 - core), False)
        to_sib(zz).start()

    loop(Z, give_sib)

    def to_z(zz):
        return remote(z_send.at[zz], z_in.at[z], zz_s.at[zz], zz_r.at[z], r, zz * 2 + core)

    def to_z_scale(zz):
        return remote(z_send_scale.at[zz], z_in_scale.at[z], zs_s.at[zz], zs_r.at[z], r, zz * 2 + core)

    def chip_sum(zz):
        pick(z_sum, fwd, 0, zz * 2 + core, False)
        to_sib(zz).wait_recv()
        return z_sum[...] + sib_in[zz]

    def give_z(k):
        zz = (z + 1 + k) % Z
        z_send[zz], z_send_scale[zz] = code(chip_sum(zz))
        to_z(zz).start()
        to_z_scale(zz).start()

    loop(Z - 1, give_z)
    gram[2]()

    loop(Z, lambda zz: sib_arrival(zz).wait_recv())

    def mirror(s):
        left = rowp[index_ref[s, 0] % C]
        mir[s] = jnp.dot(left, tile_buf[s], preferred_element_type=F32)

    loop(S, mirror)

    gram[3]()

    def to_row(peer):
        return remote(col_send.at[peer], col_in.at[r], cc_s.at[peer], cc_r.at[r], peer, c)

    def to_row_scale(peer):
        return remote(col_send_scale.at[peer], col_in_scale.at[r], cs_s.at[peer], cs_r.at[r], peer, c)

    def give_row(k):
        peer = (r + 1 + k) % R
        pick(z_sum, mir, 1, peer, True)
        col_send[peer], col_send_scale[peer] = code(z_sum[...])
        to_row(peer).start()
        to_row_scale(peer).start()

    loop(R - 1, give_row)
    out_ref[...] = self_ref[...] * probe_ref[...].astype(F32) + chip_sum(z)
    pick(z_sum, mir, 1, r, True)
    out_ref[...] += z_sum[...]
    gram[4]()

    sums = g4[...].reshape(-1, 2 * K)
    gram_blocks = {}
    lanes = lane_of((K, 2 * K))
    down = lax.broadcasted_iota(jnp.int32, (K, 2 * K), 0)
    eye = jnp.where(lanes == down + K, 1.0, 0.0)
    for i, (b, a) in enumerate(pairs):
        packed = sums[i * half : (i + 1) * half]
        if a == b:
            whole = jnp.concatenate([packed, pltpu.roll(packed, K, 1)], axis=0)
            aug[b] = jnp.where(lanes < K, whole, eye)
        else:
            gram_blocks[b, a] = unpack(packed)

    all_lanes = lane_of((B, K, 2 * K))
    all_down = lax.broadcasted_iota(jnp.int32, (B, K, 2 * K), 1)
    row_lanes = lane_of((B, 1, 2 * K))

    def eliminate(k):
        whole = aug[...]
        row = aug[:, pl.ds(k, 1), :]
        column = jnp.sum(jnp.where(all_lanes == k, whole, 0.0), axis=2, keepdims=True)
        pivot = jnp.sum(jnp.where(row_lanes == k, row, 0.0), axis=2, keepdims=True)
        scaled = row / pivot
        aug[...] = jnp.where(all_down == k, scaled, whole - column * scaled)

    loop(K, eliminate)
    square = jnp.where(lane_of((K, K)) == lax.broadcasted_iota(jnp.int32, (K, K), 0), 1.0, 0.0)
    for b in range(B):
        line = [square]
        if b > 0:
            row = jnp.concatenate([gram_blocks[b, a] for a in range(b)], axis=1)
            done = solver[: b * K, : b * K]
            line = [-jnp.dot(row, done, precision=HIGH, preferred_element_type=F32), square]
        if b < B - 1:
            line.append(jnp.zeros((K, (B - 1 - b) * K), F32))
        inverse = pltpu.roll(aug[b], K, 1)[:, :K]
        solver[b * K : (b + 1) * K, :] = jnp.dot(
            inverse, jnp.concatenate(line, axis=1), precision=HIGH, preferred_element_type=F32
        )

    def add_row(k):
        peer = (r + 1 + k) % R
        remote(col_in.at[peer], col_in.at[peer], cc_s.at[peer], cc_r.at[peer], peer, c).wait_recv()
        lines = col_in_scale.at[peer]
        remote(lines, lines, cs_s.at[peer], cs_r.at[peer], peer, c).wait_recv()
        out_ref[...] += decode(col_in[peer], col_in_scale[peer])

    loop(R - 1, add_row)

    def add_z(k):
        peer = (z + 1 + k) % Z
        remote(z_in.at[peer], z_in.at[peer], zz_s.at[peer], zz_r.at[peer], r, peer * 2 + core).wait_recv()
        lines = z_in_scale.at[peer]
        remote(lines, lines, zs_s.at[peer], zs_r.at[peer], r, peer * 2 + core).wait_recv()
        out_ref[...] += decode(z_in[peer], z_in_scale[peer])

    loop(Z - 1, add_z)

    product = out_ref[...]
    inner = jnp.zeros((B * K, 2 * K), F32)
    for part in split3(product)[::-1]:
        both = jnp.concatenate([part, part], axis=0)
        inner = inner + lax.dot_general(basis[...], both, NT, preferred_element_type=F32)
    for b in range(B):
        h_buf[b * half : (b + 1) * half, :] = pack(inner[b * K : (b + 1) * K])
    reduce_along()
    targets = h3[...].reshape(-1, 2 * K)
    stacked = jnp.concatenate([unpack(targets[b * half : (b + 1) * half]) for b in range(B)], axis=0)
    solved = jnp.dot(solver[...], stacked, precision=HIGH, preferred_element_type=F32)
    coef_ref[...] = solved.reshape(B, K, K)

    gram[5]()
    loop(C - 1, lambda k: a1(k).wait_send())
    loop(R - 1, lambda k: a2(k).wait_send())
    loop(C - 1, lambda k: a3(k).wait_send())
    loop(R - 1, lambda k: row_gather(k).wait_send())
    loop(Z - 1, lambda k: z_gather(k).wait_send())
    loop(Z, lambda zz: sib_gather(zz).wait_send())
    loop(Z, lambda zz: to_sib(zz).wait_send())
    loop(Z - 1, lambda k: to_z((z + 1 + k) % Z).wait_send())
    loop(Z - 1, lambda k: to_z_scale((z + 1 + k) % Z).wait_send())
    loop(R - 1, lambda k: to_row((r + 1 + k) % R).wait_send())
    loop(R - 1, lambda k: to_row_scale((r + 1 + k) % R).wait_send())


def finish(product_ref, coef_ref, prior_ref, probe_ref, out_ref, coef_out):
    B, K, _ = coef_ref.shape
    coef_out[...] = coef_ref[...]
    stacked = coef_ref[...].reshape(B * K, K)
    last = (B - 1) * K
    taken = jnp.zeros(out_ref.shape, F32)
    for part in split3(stacked.T)[::-1]:
        for b in range(B - 1):
            taken = taken + jnp.dot(part[:, b * K : (b + 1) * K], prior_ref[b], preferred_element_type=F32)
        taken = taken + jnp.dot(part[:, last:], probe_ref[...], preferred_element_type=F32)
    out_ref[...] = product_ref[...] - taken


def shards(R, C, probe_block, prior_blocks, self_relatedness, tile_values, tile_index):
    K, T = probe_block.shape
    S = tile_values.shape[0]
    B = prior_blocks.shape[0] + 1
    Z = C // 2
    half = K // 2
    g_rows = round_up(-(-(B * (B + 1) // 2 * half) // (R * C)), 8)
    h_rows = round_up(-(-(B * half) // C), 8)
    vmem = lambda shape, dtype=F32: pltpu.VMEM(shape, dtype)
    dma = lambda *shape: pltpu.SemaphoreType.DMA(shape)
    W = 2 * K

    def reduce_scratch(rows):
        return [
            vmem((R * C * rows, W)), vmem((R, C * rows, W)), vmem((C * rows, W)),
            vmem((C, rows, W)), vmem((C, rows, W)), vmem((R, C, rows, W)),
        ]

    scratch = [
        pltpu.SMEM(tile_index.shape, jnp.int32), vmem((S, T, T), BF16), vmem((B * K, T), BF16), vmem((C, K, T), BF16), vmem((R, K, T), BF16),
        vmem((S, K, T)), vmem((S, K, T)),
        vmem((Z, K, T)), vmem((Z, K, T)), vmem((K, T)),
        vmem((Z, K, T), I16), vmem((Z, K, T), I16), vmem((Z, 8, 128)), vmem((Z, 8, 128)),
        vmem((R, K, T), I16), vmem((R, K, T), I16), vmem((R, 8, 128)), vmem((R, 8, 128)),
        *reduce_scratch(g_rows),
        vmem((C * h_rows, W)), vmem((C, h_rows, W)), vmem((R, h_rows, W)), vmem((C, h_rows, W)),
        vmem((B, K, W)), vmem((B * K, B * K)),
        pltpu.SemaphoreType.DMA, dma(S), dma(Z), dma(Z), dma(Z), dma(Z), dma(R), dma(R), dma(Z), dma(Z),
        dma(Z), dma(Z), dma(Z), dma(Z), dma(R), dma(R), dma(R), dma(R),
        dma(2, R), dma(2, R), dma(2, C), dma(2, C), dma(R), dma(R), dma(2, C), dma(2, C),
    ]
    in_vmem = pl.BlockSpec(memory_space=pltpu.VMEM)
    product, coefficients = pl.pallas_call(
        functools.partial(kernel, R, C, S, B, K, g_rows, h_rows),
        out_shape=(jax.ShapeDtypeStruct((K, T), F32), jax.ShapeDtypeStruct((B, K, K), F32)),
        in_specs=[
            pl.BlockSpec(memory_space=pl.ANY), in_vmem, in_vmem, in_vmem, pl.BlockSpec(memory_space=pl.ANY),
        ],
        out_specs=(in_vmem, in_vmem),
        scratch_shapes=scratch,
        compiler_params=pltpu.CompilerParams(
            collective_id=0, has_side_effects=True, vmem_limit_bytes=56 * 1024 * 1024
        ),
        cost_estimate=pl.CostEstimate(
            flops=4 * S * K * T * T, bytes_accessed=2 * S * T * T, transcendentals=0
        ),
    )(tile_index, probe_block, prior_blocks, self_relatedness[None], tile_values)
    return pl.pallas_call(
        finish,
        out_shape=(jax.ShapeDtypeStruct((K, T), F32), jax.ShapeDtypeStruct((B, K, K), F32)),
        in_specs=[in_vmem] * 4,
        out_specs=(in_vmem, in_vmem),
    )(product, coefficients, prior_blocks, probe_block)


def solution(mesh):
    in_specs = (
        P(None, ("row", "col")),
        P(None, None, ("row", "col")),
        P(("row", "col")),
        P(("row", "col"), None, None),
        P(("row", "col"), None),
    )
    out_specs = (P(None, ("row", "col")), P())
    body = functools.partial(shards, mesh.shape["row"], mesh.shape["col"])
    return jax.shard_map(body, mesh=mesh, in_specs=in_specs, out_specs=out_specs, check_vma=False)
```

```python
import functools

import jax
import jax.numpy as jnp
from jax import lax
from jax.experimental import pallas as pl
from jax.experimental.pallas import tpu as pltpu
from jax.sharding import PartitionSpec as P

HIGH = lax.Precision.HIGHEST
MESH = pl.DeviceIdType.MESH
F32 = jnp.float32
BF16 = jnp.bfloat16
I16 = jnp.int16
NT = (((1,), (1,)), ((), ()))


def round_up(value, unit):
    return -(-value // unit) * unit


def split3(x):
    hi = x.astype(BF16)
    rest = x - hi.astype(F32)
    mid = rest.astype(BF16)
    lo = (rest - mid.astype(F32)).astype(BF16)
    return hi, mid, lo


def lane_of(shape):
    return lax.broadcasted_iota(jnp.int32, shape, len(shape) - 1)


def pack(block):
    half = block.shape[0] // 2
    return jnp.where(lane_of((half, block.shape[1])) < block.shape[1] // 2, block[:half], block[half:])


def unpack(packed):
    width = packed.shape[1] // 2
    return jnp.concatenate([packed[:, :width], pltpu.roll(packed, width, 1)[:, :width]], axis=0)


def code(block):
    rows = block.shape[0]
    most = jnp.maximum(jnp.max(jnp.abs(block), axis=1, keepdims=True), 1e-30)
    quantized = jnp.round(block * (32767.0 / most)).astype(jnp.int32).astype(jnp.int16)
    shape = (rows, 128)
    hit = lane_of(shape) == lax.broadcasted_iota(jnp.int32, shape, 0)
    line = jnp.sum(jnp.where(hit, most * (1.0 / 32767.0), 0.0), axis=0, keepdims=True)
    return quantized, jnp.broadcast_to(line, (8, 128))


def decode(quantized, lines):
    shape = (quantized.shape[0], 128)
    hit = lane_of(shape) == lax.broadcasted_iota(jnp.int32, shape, 0)
    scale = jnp.sum(jnp.where(hit, lines[:1], 0.0), axis=1, keepdims=True)
    return quantized.astype(jnp.int32).astype(F32) * scale


def kernel(
    R, C, S, B, K, g_rows, h_rows,
    index_in, probe_ref, prior_ref, self_ref, tiles_ref,
    out_ref, coef_ref,
    index_ref, tile_buf, basis, rowp, colp, fwd, mir, row_part, sib_in, z_sum, z_send, z_in, z_send_scale, z_in_scale,
    col_send, col_in, col_send_scale, col_in_scale,
    g_buf, g1, g2, g2_in, g3, g4, h_buf, h1, h2, h3, aug, solver,
    index_sem, prior_sem, tile_sem, gz_s, gz_r, gs_s, gs_r, gr_s, gr_r, sb_s, sb_r, zz_s, zz_r, zs_s, zs_r, cc_s, cc_r, cs_s, cs_r,
    red_row_s, red_row_r, red_col_s, red_col_r, al_row_s, al_row_r, al_col_s, al_col_r,
):
    Z = C // 2
    r, c = lax.axis_index("row"), lax.axis_index("col")
    z, core = c // 2, c % 2
    sib = z * 2 + (1 - core)
    pairs = [(b, a) for a in range(B) for b in range(a, B)]

    def local(s):
        return pltpu.make_async_copy(tiles_ref.at[s], tile_buf.at[s], tile_sem.at[s])

    def remote(src, dst, ssem, rsem, row, col):
        return pltpu.make_async_remote_copy(
            src_ref=src, dst_ref=dst, send_sem=ssem, recv_sem=rsem, device_id=(row, col), device_id_type=MESH
        )

    def loop(n, body):
        def step(k, carry):
            body(k)
            return carry

        lax.fori_loop(0, n, step, 0)

    index_copy = pltpu.make_async_copy(index_in, index_ref, index_sem)
    index_copy.start()
    prior_copies = [
        pltpu.make_async_copy(prior_ref.at[b], basis.at[pl.ds(b * K, K)], prior_sem.at[b]) for b in range(B - 1)
    ]
    for copy in prior_copies:
        copy.start()
    loop(S, lambda s: local(s).start())

    barrier = pltpu.get_barrier_semaphore()
    loop(C - 1, lambda k: pl.semaphore_signal(barrier, inc=1, device_id=(r, (c + 1 + k) % C), device_id_type=MESH))
    loop(R - 1, lambda k: pl.semaphore_signal(barrier, inc=1, device_id=((r + 1 + k) % R, c), device_id_type=MESH))
    pl.semaphore_wait(barrier, C + R - 2)

    def row_gather(k):
        peer = (r + 1 + k) % R
        return remote(probe_ref, colp.at[r], gr_s.at[peer], gr_r.at[r], peer, c)

    def z_gather(k):
        peer = (z + 1 + k) % Z
        return remote(probe_ref, rowp.at[c], gz_s.at[peer], gz_r.at[z], r, peer * 2 + core)

    def sib_gather(zz):
        slot = zz * 2 + core
        return remote(rowp.at[slot], rowp.at[slot], gs_s.at[zz], gs_r.at[zz], r, sib)

    def sib_arrival(zz):
        slot = zz * 2 + (1 - core)
        return remote(rowp.at[slot], rowp.at[slot], gs_s.at[zz], gs_r.at[zz], r, sib)

    loop(R - 1, lambda k: row_gather(k).start())
    loop(Z - 1, lambda k: z_gather(k).start())
    rowp[c] = probe_ref[...]
    colp[r] = probe_ref[...]
    sib_gather(z).start()

    def reducer(buf, in1, buf2, in2, all3, all4, rows):
        chunk = C * rows

        def p1(k):
            peer = (r + 1 + k) % R
            src = buf.at[pl.ds(pl.multiple_of(peer * chunk, 8), chunk)]
            return remote(src, in1.at[r], red_row_s.at[0, peer], red_row_r.at[0, r], peer, c)

        def p2(k):
            peer = (c + 1 + k) % C
            src = buf2.at[pl.ds(pl.multiple_of(peer * rows, 8), rows)]
            return remote(src, in2.at[c], red_col_s.at[0, peer], red_col_r.at[0, c], r, peer)

        def p3(k):
            peer = (c + 1 + k) % C
            return remote(all3.at[c], all3.at[c], red_col_s.at[1, peer], red_col_r.at[1, c], r, peer)

        def p4(k):
            peer = (r + 1 + k) % R
            return remote(all3, all4.at[r], red_row_s.at[1, peer], red_row_r.at[1, r], peer, c)

        def got_row(phase, dst, k):
            peer = (r + 1 + k) % R
            remote(dst.at[peer], dst.at[peer], red_row_s.at[phase, peer], red_row_r.at[phase, peer], peer, c).wait_recv()

        def got_col(phase, dst, k):
            peer = (c + 1 + k) % C
            remote(dst.at[peer], dst.at[peer], red_col_s.at[phase, peer], red_col_r.at[phase, peer], r, peer).wait_recv()

        def first():
            loop(R - 1, lambda k: p1(k).start())

        def second():
            buf2[...] = buf[pl.ds(pl.multiple_of(r * chunk, 8), chunk), :]

            def add(k):
                got_row(0, in1, k)
                buf2[...] += in1[(r + 1 + k) % R]

            loop(R - 1, add)
            loop(C - 1, lambda k: p2(k).start())

        def third():
            def add(k, total):
                got_col(0, in2, k)
                return total + in2[(c + 1 + k) % C]

            all3[c] = lax.fori_loop(0, C - 1, add, buf2[pl.ds(pl.multiple_of(c * rows, 8), rows), :])
            loop(C - 1, lambda k: p3(k).start())

        def fourth():
            loop(C - 1, lambda k: got_col(1, all3, k))
            loop(R - 1, lambda k: p4(k).start())
            all4[r] = all3[...]

        def fifth():
            loop(R - 1, lambda k: got_row(1, all4, k))

        def drain():
            loop(R - 1, lambda k: p1(k).wait_send())
            loop(C - 1, lambda k: p2(k).wait_send())
            loop(C - 1, lambda k: p3(k).wait_send())
            loop(R - 1, lambda k: p4(k).wait_send())

        return first, second, third, fourth, fifth, drain

    gram = reducer(g_buf, g1, g2, g2_in, g3, g4, g_rows)

    def a1(k):
        peer = (c + 1 + k) % C
        src = h_buf.at[pl.ds(pl.multiple_of(peer * h_rows, 8), h_rows)]
        return remote(src, h1.at[c], al_col_s.at[0, peer], al_col_r.at[0, c], r, peer)

    def a2(k):
        peer = (r + 1 + k) % R
        return remote(h2.at[r], h2.at[r], al_row_s.at[peer], al_row_r.at[r], peer, c)

    def a3(k):
        peer = (c + 1 + k) % C
        return remote(h3.at[c], h3.at[c], al_col_s.at[1, peer], al_col_r.at[1, c], r, peer)

    def got_a_col(phase, dst, k):
        peer = (c + 1 + k) % C
        remote(dst.at[peer], dst.at[peer], al_col_s.at[phase, peer], al_col_r.at[phase, peer], r, peer).wait_recv()

    def got_a_row(k):
        peer = (r + 1 + k) % R
        remote(h2.at[peer], h2.at[peer], al_row_s.at[peer], al_row_r.at[peer], peer, c).wait_recv()

    def along_parts():
        loop(C - 1, lambda k: a1(k).start())

    def along_sums():
        def add(k, total):
            got_a_col(0, h1, k)
            return total + h1[(c + 1 + k) % C]

        h2[r] = lax.fori_loop(0, C - 1, add, h_buf[pl.ds(pl.multiple_of(c * h_rows, 8), h_rows), :])
        loop(R - 1, lambda k: a2(k).start())

    def along_totals():
        loop(R - 1, got_a_row)
        h3[c] = lax.fori_loop(1, R, lambda k, total: total + h2[k], h2[0])
        loop(C - 1, lambda k: a3(k).start())

    def along_done():
        loop(C - 1, lambda k: got_a_col(1, h3, k))

    for copy in prior_copies:
        copy.wait()
    basis[(B - 1) * K :, :] = probe_ref[...]
    half = K // 2
    used = len(pairs) * half
    spot = 0
    for a in range(B):
        one = basis[a * K : (a + 1) * K, :]
        both = jnp.concatenate([one, one], axis=0)
        blocks = lax.dot_general(basis[a * K :, :], both, NT, preferred_element_type=F32)
        for b in range(a, B):
            g_buf[spot : spot + half, :] = pack(blocks[(b - a) * K : (b - a + 1) * K])
            spot += half
    if g_buf.shape[0] > used:
        g_buf[used:, :] = jnp.zeros((g_buf.shape[0] - used, 2 * K), F32)
    if h_buf.shape[0] > B * half:
        h_buf[B * half :, :] = jnp.zeros((h_buf.shape[0] - B * half, 2 * K), F32)
    gram[0]()

    def got_row_probe(k):
        peer = (r + 1 + k) % R
        remote(colp.at[peer], colp.at[peer], gr_s.at[peer], gr_r.at[peer], peer, c).wait_recv()

    loop(R - 1, got_row_probe)
    index_copy.wait()

    def forward(s):
        local(s).wait()
        right = colp[index_ref[1, s] // C]
        fwd[s] = lax.dot_general(tile_buf[s], right, NT, preferred_element_type=F32).T

    loop(S, forward)
    gram[1]()

    def pick(dst, parts, column, number, divide):
        hits = []
        for slot in range(S):
            value = index_ref[column, slot]
            place = value // C if divide else value % C
            hits.append(jnp.logical_and(place == number, index_ref[2, slot] > 0))

        def some(k):
            rows = pl.ds(pl.multiple_of(k * 16, 16), 16)
            total = jnp.where(hits[0], parts[0, rows, :], 0.0)
            for slot in range(1, S):
                total = total + jnp.where(hits[slot], parts[slot, rows, :], 0.0)
            dst[rows, :] = total

        loop(K // 16, some)

    def to_sib(zz):
        return remote(row_part.at[zz], sib_in.at[zz], sb_s.at[zz], sb_r.at[zz], r, sib)

    def give_sib(k):
        zz = (z + 1 + k) % Z
        pick(row_part.at[zz], fwd, 0, zz * 2 + (1 - core), False)
        to_sib(zz).start()

    loop(Z, give_sib)

    def share_probe(k):
        peer = (z + 1 + k) % Z
        slot = peer * 2 + core
        remote(rowp.at[slot], rowp.at[slot], gz_s.at[peer], gz_r.at[peer], r, slot).wait_recv()
        sib_gather(peer).start()

    loop(Z - 1, share_probe)
    gram[2]()

    def to_z(zz):
        return remote(z_send.at[zz], z_in.at[z], zz_s.at[zz], zz_r.at[z], r, zz * 2 + core)

    def to_z_scale(zz):
        return remote(z_send_scale.at[zz], z_in_scale.at[z], zs_s.at[zz], zs_r.at[z], r, zz * 2 + core)

    def chip_sum(zz):
        pick(z_sum, fwd, 0, zz * 2 + core, False)
        to_sib(zz).wait_recv()
        return z_sum[...] + sib_in[zz]

    def give_z(k):
        zz = (z + 1 + k) % Z
        z_send[zz], z_send_scale[zz] = code(chip_sum(zz))
        to_z(zz).start()
        to_z_scale(zz).start()

    loop(Z - 1, give_z)
    gram[3]()

    loop(Z, lambda zz: sib_arrival(zz).wait_recv())

    gram[4]()

    sums = g4[...].reshape(-1, 2 * K)
    gram_blocks = {}
    lanes = lane_of((K, 2 * K))
    down = lax.broadcasted_iota(jnp.int32, (K, 2 * K), 0)
    eye = jnp.where(lanes == down + K, 1.0, 0.0)
    for i, (b, a) in enumerate(pairs):
        packed = sums[i * half : (i + 1) * half]
        if a == b:
            whole = jnp.concatenate([packed, pltpu.roll(packed, K, 1)], axis=0)
            aug[b] = jnp.where(lanes < K, whole, eye)
        else:
            gram_blocks[b, a] = unpack(packed)

    all_lanes = lane_of((B, K, 2 * K))
    all_down = lax.broadcasted_iota(jnp.int32, (B, K, 2 * K), 1)
    row_lanes = lane_of((B, 1, 2 * K))

    def eliminate(k):
        whole = aug[...]
        row = aug[:, pl.ds(k, 1), :]
        column = jnp.sum(jnp.where(all_lanes == k, whole, 0.0), axis=2, keepdims=True)
        pivot = jnp.sum(jnp.where(row_lanes == k, row, 0.0), axis=2, keepdims=True)
        scaled = row / pivot
        aug[...] = jnp.where(all_down == k, scaled, whole - column * scaled)

    wide = 256
    pieces = S * (out_ref.shape[1] // wide)
    steps = 2 if 2 * pieces <= K else K // pieces

    def mirror(i):
        s = i // (pieces // S)
        columns = pl.ds(pl.multiple_of(i % (pieces // S) * wide, wide), wide)
        left = rowp[index_ref[0, s] % C]
        mir[s, :, columns] = jnp.dot(left, tile_buf[s, :, columns], preferred_element_type=F32)
        for step in range(steps):
            eliminate(i * steps + step)

    loop(pieces, mirror)

    def to_row(peer):
        return remote(col_send.at[peer], col_in.at[r], cc_s.at[peer], cc_r.at[r], peer, c)

    def to_row_scale(peer):
        return remote(col_send_scale.at[peer], col_in_scale.at[r], cs_s.at[peer], cs_r.at[r], peer, c)

    def give_row(k):
        peer = (r + 1 + k) % R
        pick(z_sum, mir, 1, peer, True)
        col_send[peer], col_send_scale[peer] = code(z_sum[...])
        to_row(peer).start()
        to_row_scale(peer).start()

    loop(R - 1, give_row)
    out_ref[...] = self_ref[...] * probe_ref[...].astype(F32) + chip_sum(z)
    pick(z_sum, mir, 1, r, True)
    out_ref[...] += z_sum[...]

    loop(K - steps * pieces, lambda k: eliminate(steps * pieces + k))

    inverse = [pltpu.roll(aug[b], K, 1)[:, :K] for b in range(B)]

    def solver_row(b):
        line = [inverse[b]]
        if b > 0:
            row = jnp.concatenate([gram_blocks[b, a] for a in range(b)], axis=1)
            scaled = jnp.dot(inverse[b], row, precision=HIGH, preferred_element_type=F32)
            done = solver[: b * K, : b * K]
            line = [-jnp.dot(scaled, done, precision=HIGH, preferred_element_type=F32), inverse[b]]
        if b < B - 1:
            line.append(jnp.zeros((K, (B - 1 - b) * K), F32))
        solver[b * K : (b + 1) * K, :] = jnp.concatenate(line, axis=1)

    def add_row(k):
        peer = (r + 1 + k) % R
        remote(col_in.at[peer], col_in.at[peer], cc_s.at[peer], cc_r.at[peer], peer, c).wait_recv()
        lines = col_in_scale.at[peer]
        remote(lines, lines, cs_s.at[peer], cs_r.at[peer], peer, c).wait_recv()
        out_ref[...] += decode(col_in[peer], col_in_scale[peer])


    def add_z(k):
        peer = (z + 1 + k) % Z
        remote(z_in.at[peer], z_in.at[peer], zz_s.at[peer], zz_r.at[peer], r, peer * 2 + core).wait_recv()
        lines = z_in_scale.at[peer]
        remote(lines, lines, zs_s.at[peer], zs_r.at[peer], r, peer * 2 + core).wait_recv()
        out_ref[...] += decode(z_in[peer], z_in_scale[peer])

    loop(Z - 1, add_z)
    loop(R - 1, add_row)

    product = out_ref[...]
    inner = jnp.zeros((B * K, 2 * K), F32)
    for part in split3(product)[::-1]:
        both = jnp.concatenate([part, part], axis=0)
        inner = inner + lax.dot_general(basis[...], both, NT, preferred_element_type=F32)
    for b in range(B):
        h_buf[b * half : (b + 1) * half, :] = pack(inner[b * K : (b + 1) * K])
    along_parts()
    for b in range(B - 2):
        solver_row(b)
    along_sums()
    solver_row(B - 2)
    along_totals()
    solver_row(B - 1)
    along_done()
    targets = h3[...].reshape(-1, 2 * K)
    stacked = jnp.concatenate([unpack(targets[b * half : (b + 1) * half]) for b in range(B)], axis=0)
    solved = jnp.dot(solver[...], stacked, precision=HIGH, preferred_element_type=F32)
    coef_ref[...] = solved.reshape(B, K, K)

    gram[5]()
    loop(C - 1, lambda k: a1(k).wait_send())
    loop(R - 1, lambda k: a2(k).wait_send())
    loop(C - 1, lambda k: a3(k).wait_send())
    loop(R - 1, lambda k: row_gather(k).wait_send())
    loop(Z - 1, lambda k: z_gather(k).wait_send())
    loop(Z, lambda zz: sib_gather(zz).wait_send())
    loop(Z, lambda zz: to_sib(zz).wait_send())
    loop(Z - 1, lambda k: to_z((z + 1 + k) % Z).wait_send())
    loop(Z - 1, lambda k: to_z_scale((z + 1 + k) % Z).wait_send())
    loop(R - 1, lambda k: to_row((r + 1 + k) % R).wait_send())
    loop(R - 1, lambda k: to_row_scale((r + 1 + k) % R).wait_send())


def finish(product_ref, coef_ref, prior_ref, probe_ref, out_ref, coef_out):
    B, K, _ = coef_ref.shape
    coef_out[...] = coef_ref[...]
    stacked = coef_ref[...].reshape(B * K, K)
    last = (B - 1) * K
    taken = jnp.zeros(out_ref.shape, F32)
    for part in split3(stacked.T)[::-1]:
        for b in range(B - 1):
            taken = taken + jnp.dot(part[:, b * K : (b + 1) * K], prior_ref[b], preferred_element_type=F32)
        taken = taken + jnp.dot(part[:, last:], probe_ref[...], preferred_element_type=F32)
    out_ref[...] = product_ref[...] - taken


def shards(R, C, probe_block, prior_blocks, self_relatedness, tile_values, tile_index):
    K, T = probe_block.shape
    S = tile_values.shape[0]
    B = prior_blocks.shape[0] + 1
    Z = C // 2
    half = K // 2
    g_rows = round_up(-(-(B * (B + 1) // 2 * half) // (R * C)), 8)
    h_rows = round_up(-(-(B * half) // C), 8)
    vmem = lambda shape, dtype=F32: pltpu.VMEM(shape, dtype)
    dma = lambda *shape: pltpu.SemaphoreType.DMA(shape)
    W = 2 * K

    def reduce_scratch(rows):
        return [
            vmem((R * C * rows, W)), vmem((R, C * rows, W)), vmem((C * rows, W)),
            vmem((C, rows, W)), vmem((C, rows, W)), vmem((R, C, rows, W)),
        ]

    scratch = [
        pltpu.SMEM(tile_index.shape[::-1], jnp.int32), vmem((S, T, T), BF16), vmem((B * K, T), BF16), vmem((C, K, T), BF16), vmem((R, K, T), BF16),
        vmem((S, K, T)), vmem((S, K, T)),
        vmem((Z, K, T)), vmem((Z, K, T)), vmem((K, T)),
        vmem((Z, K, T), I16), vmem((Z, K, T), I16), vmem((Z, 8, 128)), vmem((Z, 8, 128)),
        vmem((R, K, T), I16), vmem((R, K, T), I16), vmem((R, 8, 128)), vmem((R, 8, 128)),
        *reduce_scratch(g_rows),
        vmem((C * h_rows, W)), vmem((C, h_rows, W)), vmem((R, h_rows, W)), vmem((C, h_rows, W)),
        vmem((B, K, W)), vmem((B * K, B * K)),
        pltpu.SemaphoreType.DMA, dma(B - 1), dma(S), dma(Z), dma(Z), dma(Z), dma(Z), dma(R), dma(R), dma(Z), dma(Z),
        dma(Z), dma(Z), dma(Z), dma(Z), dma(R), dma(R), dma(R), dma(R),
        dma(2, R), dma(2, R), dma(2, C), dma(2, C), dma(R), dma(R), dma(2, C), dma(2, C),
    ]
    in_vmem = pl.BlockSpec(memory_space=pltpu.VMEM)
    in_any = pl.BlockSpec(memory_space=pl.ANY)
    product, coefficients = pl.pallas_call(
        functools.partial(kernel, R, C, S, B, K, g_rows, h_rows),
        out_shape=(jax.ShapeDtypeStruct((K, T), F32), jax.ShapeDtypeStruct((B, K, K), F32)),
        in_specs=[
            in_any, in_vmem, in_any, in_vmem, in_any,
        ],
        out_specs=(in_vmem, in_vmem),
        scratch_shapes=scratch,
        compiler_params=pltpu.CompilerParams(
            collective_id=0, has_side_effects=True, vmem_limit_bytes=56 * 1024 * 1024
        ),
        cost_estimate=pl.CostEstimate(
            flops=4 * S * K * T * T, bytes_accessed=2 * S * T * T, transcendentals=0
        ),
    )(tile_index.T, probe_block, prior_blocks, self_relatedness[None], tile_values)
    return pl.pallas_call(
        finish,
        out_shape=(jax.ShapeDtypeStruct((K, T), F32), jax.ShapeDtypeStruct((B, K, K), F32)),
        in_specs=[in_vmem] * 4,
        out_specs=(in_vmem, in_vmem),
    )(product, coefficients, prior_blocks, probe_block)


def solution(mesh):
    in_specs = (
        P(None, ("row", "col")),
        P(None, None, ("row", "col")),
        P(("row", "col")),
        P(("row", "col"), None, None),
        P(("row", "col"), None),
    )
    out_specs = (P(None, ("row", "col")), P())
    body = functools.partial(shards, mesh.shape["row"], mesh.shape["col"])
    return jax.shard_map(body, mesh=mesh, in_specs=in_specs, out_specs=out_specs, check_vma=False)
```

```python
import functools

import jax
import jax.numpy as jnp
from jax import lax
from jax.experimental import pallas as pl
from jax.experimental.pallas import tpu as pltpu
from jax.sharding import PartitionSpec as P

HIGH = lax.Precision.HIGHEST
MESH = pl.DeviceIdType.MESH
F32 = jnp.float32
BF16 = jnp.bfloat16
I16 = jnp.int16
NT = (((1,), (1,)), ((), ()))


def round_up(value, unit):
    return -(-value // unit) * unit


def split3(x):
    hi = x.astype(BF16)
    rest = x - hi.astype(F32)
    mid = rest.astype(BF16)
    lo = (rest - mid.astype(F32)).astype(BF16)
    return hi, mid, lo


def lane_of(shape):
    return lax.broadcasted_iota(jnp.int32, shape, len(shape) - 1)


def pack(block):
    half = block.shape[0] // 2
    return jnp.where(lane_of((half, block.shape[1])) < block.shape[1] // 2, block[:half], block[half:])


def unpack(packed):
    width = packed.shape[1] // 2
    return jnp.concatenate([packed[:, :width], pltpu.roll(packed, width, 1)[:, :width]], axis=0)


def code(block):
    rows = block.shape[0]
    most = jnp.maximum(jnp.max(jnp.abs(block), axis=1, keepdims=True), 1e-30)
    quantized = jnp.round(block * (32767.0 / most)).astype(jnp.int32).astype(jnp.int16)
    shape = (rows, 128)
    hit = lane_of(shape) == lax.broadcasted_iota(jnp.int32, shape, 0)
    line = jnp.sum(jnp.where(hit, most * (1.0 / 32767.0), 0.0), axis=0, keepdims=True)
    return quantized, jnp.broadcast_to(line, (8, 128))


def decode(quantized, lines):
    shape = (quantized.shape[0], 128)
    hit = lane_of(shape) == lax.broadcasted_iota(jnp.int32, shape, 0)
    scale = jnp.sum(jnp.where(hit, lines[:1], 0.0), axis=1, keepdims=True)
    return quantized.astype(jnp.int32).astype(F32) * scale


def kernel(
    R, C, S, B, K, g_rows, h_rows,
    index_in, probe_ref, prior_ref, self_ref, tiles_ref,
    out_ref, coef_ref,
    index_ref, tile_buf, basis, rowp, colp, fwd, mir, row_part, sib_in, z_sum, z_send, z_in, z_send_scale, z_in_scale,
    col_send, col_in, col_send_scale, col_in_scale,
    g_buf, g1, g2, g2_in, g3, g4, h_buf, h1, h2, h3, aug, solver,
    index_sem, prior_sem, tile_sem, gz_s, gz_r, gs_s, gs_r, gr_s, gr_r, sb_s, sb_r, zz_s, zz_r, zs_s, zs_r, cc_s, cc_r, cs_s, cs_r,
    red_row_s, red_row_r, red_col_s, red_col_r, al_row_s, al_row_r, al_col_s, al_col_r,
):
    Z = C // 2
    r, c = lax.axis_index("row"), lax.axis_index("col")
    z, core = c // 2, c % 2
    sib = z * 2 + (1 - core)
    pairs = [(b, a) for a in range(B) for b in range(a, B)]

    def local(s):
        return pltpu.make_async_copy(tiles_ref.at[s], tile_buf.at[s], tile_sem.at[s])

    def remote(src, dst, ssem, rsem, row, col):
        return pltpu.make_async_remote_copy(
            src_ref=src, dst_ref=dst, send_sem=ssem, recv_sem=rsem, device_id=(row, col), device_id_type=MESH
        )

    def loop(n, body):
        def step(k, carry):
            body(k)
            return carry

        lax.fori_loop(0, n, step, 0)

    index_copy = pltpu.make_async_copy(index_in, index_ref, index_sem)
    index_copy.start()
    prior_copies = [
        pltpu.make_async_copy(prior_ref.at[b], basis.at[pl.ds(b * K, K)], prior_sem.at[b]) for b in range(B - 1)
    ]
    for copy in prior_copies:
        copy.start()
    loop(S, lambda s: local(s).start())

    barrier = pltpu.get_barrier_semaphore()
    loop(C - 1, lambda k: pl.semaphore_signal(barrier, inc=1, device_id=(r, (c + 1 + k) % C), device_id_type=MESH))
    loop(R - 1, lambda k: pl.semaphore_signal(barrier, inc=1, device_id=((r + 1 + k) % R, c), device_id_type=MESH))
    pl.semaphore_wait(barrier, C + R - 2)

    def row_gather(k):
        peer = (r + 1 + k) % R
        return remote(probe_ref, colp.at[r], gr_s.at[peer], gr_r.at[r], peer, c)

    def z_gather(k):
        peer = (z + 1 + k) % Z
        return remote(probe_ref, rowp.at[c], gz_s.at[peer], gz_r.at[z], r, peer * 2 + core)

    def sib_gather(zz):
        slot = zz * 2 + core
        return remote(rowp.at[slot], rowp.at[slot], gs_s.at[zz], gs_r.at[zz], r, sib)

    def sib_arrival(zz):
        slot = zz * 2 + (1 - core)
        return remote(rowp.at[slot], rowp.at[slot], gs_s.at[zz], gs_r.at[zz], r, sib)

    loop(R - 1, lambda k: row_gather(k).start())
    loop(Z - 1, lambda k: z_gather(k).start())
    rowp[c] = probe_ref[...]
    colp[r] = probe_ref[...]
    sib_gather(z).start()

    def reducer(buf, in1, buf2, in2, all3, all4, rows):
        chunk = C * rows

        def p1(k):
            peer = (r + 1 + k) % R
            src = buf.at[pl.ds(pl.multiple_of(peer * chunk, 8), chunk)]
            return remote(src, in1.at[r], red_row_s.at[0, peer], red_row_r.at[0, r], peer, c)

        def p2(k):
            peer = (c + 1 + k) % C
            src = buf2.at[pl.ds(pl.multiple_of(peer * rows, 8), rows)]
            return remote(src, in2.at[c], red_col_s.at[0, peer], red_col_r.at[0, c], r, peer)

        def p3(k):
            peer = (c + 1 + k) % C
            return remote(all3.at[c], all3.at[c], red_col_s.at[1, peer], red_col_r.at[1, c], r, peer)

        def p4(k):
            peer = (r + 1 + k) % R
            return remote(all3, all4.at[r], red_row_s.at[1, peer], red_row_r.at[1, r], peer, c)

        def got_row(phase, dst, k):
            peer = (r + 1 + k) % R
            remote(dst.at[peer], dst.at[peer], red_row_s.at[phase, peer], red_row_r.at[phase, peer], peer, c).wait_recv()

        def got_col(phase, dst, k):
            peer = (c + 1 + k) % C
            remote(dst.at[peer], dst.at[peer], red_col_s.at[phase, peer], red_col_r.at[phase, peer], r, peer).wait_recv()

        def first():
            loop(R - 1, lambda k: p1(k).start())

        def second():
            buf2[...] = buf[pl.ds(pl.multiple_of(r * chunk, 8), chunk), :]

            def add(k):
                got_row(0, in1, k)
                buf2[...] += in1[(r + 1 + k) % R]

            loop(R - 1, add)
            loop(C - 1, lambda k: p2(k).start())

        def third():
            def add(k, total):
                got_col(0, in2, k)
                return total + in2[(c + 1 + k) % C]

            all3[c] = lax.fori_loop(0, C - 1, add, buf2[pl.ds(pl.multiple_of(c * rows, 8), rows), :])
            loop(C - 1, lambda k: p3(k).start())

        def fourth():
            loop(C - 1, lambda k: got_col(1, all3, k))
            loop(R - 1, lambda k: p4(k).start())
            all4[r] = all3[...]

        def fifth():
            loop(R - 1, lambda k: got_row(1, all4, k))

        def drain():
            loop(R - 1, lambda k: p1(k).wait_send())
            loop(C - 1, lambda k: p2(k).wait_send())
            loop(C - 1, lambda k: p3(k).wait_send())
            loop(R - 1, lambda k: p4(k).wait_send())

        return first, second, third, fourth, fifth, drain

    gram = reducer(g_buf, g1, g2, g2_in, g3, g4, g_rows)

    def a1(k):
        peer = (c + 1 + k) % C
        src = h_buf.at[pl.ds(pl.multiple_of(peer * h_rows, 8), h_rows)]
        return remote(src, h1.at[c], al_col_s.at[0, peer], al_col_r.at[0, c], r, peer)

    def a2(k):
        peer = (r + 1 + k) % R
        return remote(h2.at[r], h2.at[r], al_row_s.at[peer], al_row_r.at[r], peer, c)

    def a3(k):
        peer = (c + 1 + k) % C
        return remote(h3.at[c], h3.at[c], al_col_s.at[1, peer], al_col_r.at[1, c], r, peer)

    def got_a_col(phase, dst, k):
        peer = (c + 1 + k) % C
        remote(dst.at[peer], dst.at[peer], al_col_s.at[phase, peer], al_col_r.at[phase, peer], r, peer).wait_recv()

    def got_a_row(k):
        peer = (r + 1 + k) % R
        remote(h2.at[peer], h2.at[peer], al_row_s.at[peer], al_row_r.at[peer], peer, c).wait_recv()

    def along_parts():
        loop(C - 1, lambda k: a1(k).start())

    def along_sums():
        def add(k, total):
            got_a_col(0, h1, k)
            return total + h1[(c + 1 + k) % C]

        h2[r] = lax.fori_loop(0, C - 1, add, h_buf[pl.ds(pl.multiple_of(c * h_rows, 8), h_rows), :])
        loop(R - 1, lambda k: a2(k).start())

    def along_totals():
        loop(R - 1, got_a_row)
        h3[c] = lax.fori_loop(1, R, lambda k, total: total + h2[k], h2[0])
        loop(C - 1, lambda k: a3(k).start())

    def along_done():
        loop(C - 1, lambda k: got_a_col(1, h3, k))

    for copy in prior_copies:
        copy.wait()
    basis[(B - 1) * K :, :] = probe_ref[...]
    half = K // 2
    used = len(pairs) * half
    spot = 0
    for a in range(B):
        one = basis[a * K : (a + 1) * K, :]
        both = jnp.concatenate([one, one], axis=0)
        blocks = lax.dot_general(basis[a * K :, :], both, NT, preferred_element_type=F32)
        for b in range(a, B):
            g_buf[spot : spot + half, :] = pack(blocks[(b - a) * K : (b - a + 1) * K])
            spot += half
    if g_buf.shape[0] > used:
        g_buf[used:, :] = jnp.zeros((g_buf.shape[0] - used, 2 * K), F32)
    if h_buf.shape[0] > B * half:
        h_buf[B * half :, :] = jnp.zeros((h_buf.shape[0] - B * half, 2 * K), F32)
    gram[0]()

    def got_row_probe(k):
        peer = (r + 1 + k) % R
        remote(colp.at[peer], colp.at[peer], gr_s.at[peer], gr_r.at[peer], peer, c).wait_recv()

    loop(R - 1, got_row_probe)
    index_copy.wait()

    def forward(s):
        local(s).wait()
        right = colp[index_ref[1, s] // C]
        fwd[s] = lax.dot_general(tile_buf[s], right, NT, preferred_element_type=F32).T

    loop(S, forward)
    gram[1]()

    def pick(dst, parts, column, number, divide):
        hits = []
        for slot in range(S):
            value = index_ref[column, slot]
            place = value // C if divide else value % C
            hits.append(jnp.logical_and(place == number, index_ref[2, slot] > 0))

        def some(k):
            rows = pl.ds(pl.multiple_of(k * 16, 16), 16)
            total = jnp.where(hits[0], parts[0, rows, :], 0.0)
            for slot in range(1, S):
                total = total + jnp.where(hits[slot], parts[slot, rows, :], 0.0)
            dst[rows, :] = total

        loop(K // 16, some)

    def to_sib(zz):
        return remote(row_part.at[zz], sib_in.at[zz], sb_s.at[zz], sb_r.at[zz], r, sib)

    def give_sib(k):
        zz = (z + 1 + k) % Z
        pick(row_part.at[zz], fwd, 0, zz * 2 + (1 - core), False)
        to_sib(zz).start()

    loop(Z, give_sib)

    def share_probe(k):
        peer = (z + 1 + k) % Z
        slot = peer * 2 + core
        remote(rowp.at[slot], rowp.at[slot], gz_s.at[peer], gz_r.at[peer], r, slot).wait_recv()
        sib_gather(peer).start()

    loop(Z - 1, share_probe)
    gram[2]()

    def to_z(zz):
        return remote(z_send.at[zz], z_in.at[z], zz_s.at[zz], zz_r.at[z], r, zz * 2 + core)

    def to_z_scale(zz):
        return remote(z_send_scale.at[zz], z_in_scale.at[z], zs_s.at[zz], zs_r.at[z], r, zz * 2 + core)

    def chip_sum(zz):
        pick(z_sum, fwd, 0, zz * 2 + core, False)
        to_sib(zz).wait_recv()
        return z_sum[...] + sib_in[zz]

    def give_z(k):
        zz = (z + 1 + k) % Z
        z_send[zz], z_send_scale[zz] = code(chip_sum(zz))
        to_z(zz).start()
        to_z_scale(zz).start()

    loop(Z - 1, give_z)
    gram[3]()

    loop(Z, lambda zz: sib_arrival(zz).wait_recv())

    gram[4]()

    sums = g4[...].reshape(-1, 2 * K)
    gram_blocks = {}
    lanes = lane_of((K, 2 * K))
    down = lax.broadcasted_iota(jnp.int32, (K, 2 * K), 0)
    eye = jnp.where(lanes == down + K, 1.0, 0.0)
    for i, (b, a) in enumerate(pairs):
        packed = sums[i * half : (i + 1) * half]
        if a == b:
            whole = jnp.concatenate([packed, pltpu.roll(packed, K, 1)], axis=0)
            aug[b] = jnp.where(lanes < K, whole, eye)
        else:
            gram_blocks[b, a] = unpack(packed)

    all_lanes = lane_of((B, K, 2 * K))
    all_down = lax.broadcasted_iota(jnp.int32, (B, K, 2 * K), 1)
    row_lanes = lane_of((B, 1, 2 * K))

    def eliminate(k):
        whole = aug[...]
        row = aug[:, pl.ds(k, 1), :]
        column = jnp.sum(jnp.where(all_lanes == k, whole, 0.0), axis=2, keepdims=True)
        pivot = jnp.sum(jnp.where(row_lanes == k, row, 0.0), axis=2, keepdims=True)
        scaled = row / pivot
        aug[...] = jnp.where(all_down == k, scaled, whole - column * scaled)

    Q, wide = col_send.shape[1], col_send.shape[3]
    given = 2 if Q * (2 * S + 2 * (R - 1)) <= K else 0
    per_chunk = 2 * S + given * (R - 1)

    def to_row(peer, q):
        return remote(col_send.at[peer, q], col_in.at[r, q], cc_s.at[peer, q], cc_r.at[r, q], peer, c)

    def to_row_scale(peer, q):
        return remote(
            col_send_scale.at[peer, q], col_in_scale.at[r, q], cs_s.at[peer, q], cs_r.at[r, q], peer, c
        )

    def chunk(q):
        columns = pl.ds(pl.multiple_of(q * wide, wide), wide)

        def mirror(s):
            left = rowp[index_ref[0, s] % C]
            mir[s, :, columns] = jnp.dot(left, tile_buf[s, :, columns], preferred_element_type=F32)
            for step in range(2):
                eliminate(q * per_chunk + 2 * s + step)

        loop(S, mirror)

        def give_row(k):
            peer = (r + 1 + k) % R
            total = jnp.zeros((K, wide), F32)
            for slot in range(S):
                hit = jnp.logical_and(index_ref[1, slot] // C == peer, index_ref[2, slot] > 0)
                total = total + jnp.where(hit, mir[slot, :, columns], 0.0)
            col_send[peer, q], col_send_scale[peer, q] = code(total)
            to_row(peer, q).start()
            to_row_scale(peer, q).start()
            for step in range(given):
                eliminate(q * per_chunk + 2 * S + given * k + step)

        loop(R - 1, give_row)

    loop(Q, chunk)
    out_ref[...] = self_ref[...] * probe_ref[...].astype(F32) + chip_sum(z)
    pick(z_sum, mir, 1, r, True)
    out_ref[...] += z_sum[...]

    loop(K - Q * per_chunk, lambda k: eliminate(Q * per_chunk + k))

    inverse = [pltpu.roll(aug[b], K, 1)[:, :K] for b in range(B)]

    def solver_row(b):
        line = [inverse[b]]
        if b > 0:
            row = jnp.concatenate([gram_blocks[b, a] for a in range(b)], axis=1)
            scaled = jnp.dot(inverse[b], row, precision=HIGH, preferred_element_type=F32)
            done = solver[: b * K, : b * K]
            line = [-jnp.dot(scaled, done, precision=HIGH, preferred_element_type=F32), inverse[b]]
        if b < B - 1:
            line.append(jnp.zeros((K, (B - 1 - b) * K), F32))
        solver[b * K : (b + 1) * K, :] = jnp.concatenate(line, axis=1)

    solver_row(0)
    solver_row(1)

    def add_row(i):
        q, k = i // (R - 1), i % (R - 1)
        peer = (r + 1 + k) % R
        values, lines = col_in.at[peer, q], col_in_scale.at[peer, q]
        remote(values, values, cc_s.at[peer, q], cc_r.at[peer, q], peer, c).wait_recv()
        remote(lines, lines, cs_s.at[peer, q], cs_r.at[peer, q], peer, c).wait_recv()
        columns = pl.ds(pl.multiple_of(q * wide, wide), wide)
        out_ref[:, columns] += decode(col_in[peer, q], col_in_scale[peer, q])

    def add_z(k):
        peer = (z + 1 + k) % Z
        remote(z_in.at[peer], z_in.at[peer], zz_s.at[peer], zz_r.at[peer], r, peer * 2 + core).wait_recv()
        lines = z_in_scale.at[peer]
        remote(lines, lines, zs_s.at[peer], zs_r.at[peer], r, peer * 2 + core).wait_recv()
        out_ref[...] += decode(z_in[peer], z_in_scale[peer])

    loop(Z - 1, add_z)
    loop(Q * (R - 1), add_row)

    product = out_ref[...]
    hi, mid, lo = split3(product)
    parts = jnp.concatenate([lo, lo, mid, mid, hi, hi], axis=0)
    inner = lax.dot_general(basis[...], parts, NT, preferred_element_type=F32)
    inner = inner[:, : 2 * K] + inner[:, 2 * K : 4 * K] + inner[:, 4 * K :]
    for b in range(B):
        h_buf[b * half : (b + 1) * half, :] = pack(inner[b * K : (b + 1) * K])
    along_parts()
    for b in range(2, B - 2):
        solver_row(b)
    along_sums()
    solver_row(B - 2)
    along_totals()
    solver_row(B - 1)
    along_done()
    targets = h3[...].reshape(-1, 2 * K)
    stacked = jnp.concatenate([unpack(targets[b * half : (b + 1) * half]) for b in range(B)], axis=0)
    solved = jnp.dot(solver[...], stacked, precision=HIGH, preferred_element_type=F32)
    coef_ref[...] = solved.reshape(B, K, K)

    gram[5]()
    loop(C - 1, lambda k: a1(k).wait_send())
    loop(R - 1, lambda k: a2(k).wait_send())
    loop(C - 1, lambda k: a3(k).wait_send())
    loop(R - 1, lambda k: row_gather(k).wait_send())
    loop(Z - 1, lambda k: z_gather(k).wait_send())
    loop(Z, lambda zz: sib_gather(zz).wait_send())
    loop(Z, lambda zz: to_sib(zz).wait_send())
    loop(Z - 1, lambda k: to_z((z + 1 + k) % Z).wait_send())
    loop(Z - 1, lambda k: to_z_scale((z + 1 + k) % Z).wait_send())

    def row_left(i):
        q, k = i // (R - 1), i % (R - 1)
        to_row((r + 1 + k) % R, q).wait_send()
        to_row_scale((r + 1 + k) % R, q).wait_send()

    loop(Q * (R - 1), row_left)


def finish(product_ref, coef_ref, prior_ref, probe_ref, out_ref, coef_out):
    B, K, _ = coef_ref.shape
    coef_out[...] = coef_ref[...]
    stacked = coef_ref[...].reshape(B * K, K)
    last = (B - 1) * K
    parts = jnp.concatenate(split3(stacked.T)[::-1], axis=0)
    taken = jnp.dot(parts[:, :last], prior_ref[...].reshape(last, -1), preferred_element_type=F32)
    taken = taken + jnp.dot(parts[:, last:], probe_ref[...], preferred_element_type=F32)
    taken = taken[:K] + taken[K : 2 * K] + taken[2 * K :]
    out_ref[...] = product_ref[...] - taken


def shards(R, C, probe_block, prior_blocks, self_relatedness, tile_values, tile_index):
    K, T = probe_block.shape
    S = tile_values.shape[0]
    B = prior_blocks.shape[0] + 1
    Z = C // 2
    half = K // 2
    g_rows = round_up(-(-(B * (B + 1) // 2 * half) // (R * C)), 8)
    h_rows = round_up(-(-(B * half) // C), 8)
    vmem = lambda shape, dtype=F32: pltpu.VMEM(shape, dtype)
    dma = lambda *shape: pltpu.SemaphoreType.DMA(shape)
    W = 2 * K
    Q = T // 256

    def reduce_scratch(rows):
        return [
            vmem((R * C * rows, W)), vmem((R, C * rows, W)), vmem((C * rows, W)),
            vmem((C, rows, W)), vmem((C, rows, W)), vmem((R, C, rows, W)),
        ]

    scratch = [
        pltpu.SMEM(tile_index.shape[::-1], jnp.int32), vmem((S, T, T), BF16), vmem((B * K, T), BF16), vmem((C, K, T), BF16), vmem((R, K, T), BF16),
        vmem((S, K, T)), vmem((S, K, T)),
        vmem((Z, K, T)), vmem((Z, K, T)), vmem((K, T)),
        vmem((Z, K, T), I16), vmem((Z, K, T), I16), vmem((Z, 8, 128)), vmem((Z, 8, 128)),
        vmem((R, Q, K, T // Q), I16), vmem((R, Q, K, T // Q), I16), vmem((R, Q, 8, 128)), vmem((R, Q, 8, 128)),
        *reduce_scratch(g_rows),
        vmem((C * h_rows, W)), vmem((C, h_rows, W)), vmem((R, h_rows, W)), vmem((C, h_rows, W)),
        vmem((B, K, W)), vmem((B * K, B * K)),
        pltpu.SemaphoreType.DMA, dma(B - 1), dma(S), dma(Z), dma(Z), dma(Z), dma(Z), dma(R), dma(R), dma(Z), dma(Z),
        dma(Z), dma(Z), dma(Z), dma(Z), dma(R, Q), dma(R, Q), dma(R, Q), dma(R, Q),
        dma(2, R), dma(2, R), dma(2, C), dma(2, C), dma(R), dma(R), dma(2, C), dma(2, C),
    ]
    in_vmem = pl.BlockSpec(memory_space=pltpu.VMEM)
    in_any = pl.BlockSpec(memory_space=pl.ANY)
    product, coefficients = pl.pallas_call(
        functools.partial(kernel, R, C, S, B, K, g_rows, h_rows),
        out_shape=(jax.ShapeDtypeStruct((K, T), F32), jax.ShapeDtypeStruct((B, K, K), F32)),
        in_specs=[
            in_any, in_vmem, in_any, in_vmem, in_any,
        ],
        out_specs=(in_vmem, in_vmem),
        scratch_shapes=scratch,
        compiler_params=pltpu.CompilerParams(
            collective_id=0, has_side_effects=True, vmem_limit_bytes=56 * 1024 * 1024
        ),
        cost_estimate=pl.CostEstimate(
            flops=4 * S * K * T * T, bytes_accessed=2 * S * T * T, transcendentals=0
        ),
    )(tile_index.T, probe_block, prior_blocks, self_relatedness[None], tile_values)
    return pl.pallas_call(
        finish,
        out_shape=(jax.ShapeDtypeStruct((K, T), F32), jax.ShapeDtypeStruct((B, K, K), F32)),
        in_specs=[in_vmem] * 4,
        out_specs=(in_vmem, in_vmem),
    )(product, coefficients, prior_blocks, probe_block)


def solution(mesh):
    in_specs = (
        P(None, ("row", "col")),
        P(None, None, ("row", "col")),
        P(("row", "col")),
        P(("row", "col"), None, None),
        P(("row", "col"), None),
    )
    out_specs = (P(None, ("row", "col")), P())
    body = functools.partial(shards, mesh.shape["row"], mesh.shape["col"])
    return jax.shard_map(body, mesh=mesh, in_specs=in_specs, out_specs=out_specs, check_vma=False)
```

```python
import functools

import jax
import jax.numpy as jnp
from jax import lax
from jax.experimental import pallas as pl
from jax.experimental.pallas import tpu as pltpu
from jax.sharding import PartitionSpec as P

HIGH = lax.Precision.HIGHEST
MESH = pl.DeviceIdType.MESH
F32 = jnp.float32
BF16 = jnp.bfloat16
I16 = jnp.int16
NT = (((1,), (1,)), ((), ()))


def round_up(value, unit):
    return -(-value // unit) * unit


def split3(x):
    hi = x.astype(BF16)
    rest = x - hi.astype(F32)
    mid = rest.astype(BF16)
    lo = (rest - mid.astype(F32)).astype(BF16)
    return hi, mid, lo


def lane_of(shape):
    return lax.broadcasted_iota(jnp.int32, shape, len(shape) - 1)


def pack(block):
    half = block.shape[0] // 2
    return jnp.where(lane_of((half, block.shape[1])) < block.shape[1] // 2, block[:half], block[half:])


def unpack(packed):
    width = packed.shape[1] // 2
    return jnp.concatenate([packed[:, :width], pltpu.roll(packed, width, 1)[:, :width]], axis=0)


def code(block):
    rows = block.shape[0]
    most = jnp.maximum(jnp.max(jnp.abs(block), axis=1, keepdims=True), 1e-30)
    quantized = jnp.round(block * (32767.0 / most)).astype(jnp.int32).astype(jnp.int16)
    shape = (rows, 128)
    hit = lane_of(shape) == lax.broadcasted_iota(jnp.int32, shape, 0)
    line = jnp.sum(jnp.where(hit, most * (1.0 / 32767.0), 0.0), axis=0, keepdims=True)
    return quantized, jnp.broadcast_to(line, (8, 128))


def decode(quantized, lines):
    shape = (quantized.shape[0], 128)
    hit = lane_of(shape) == lax.broadcasted_iota(jnp.int32, shape, 0)
    scale = jnp.sum(jnp.where(hit, lines[:1], 0.0), axis=1, keepdims=True)
    return quantized.astype(jnp.int32).astype(F32) * scale


def kernel(
    R, C, S, B, K, g_rows, h_rows,
    index_in, probe_ref, prior_ref, self_ref, tiles_ref,
    out_ref, coef_ref,
    index_ref, tile_buf, basis, rowp, colp, fwd, mir, row_part, sib_in, z_sum, z_send, z_in, z_send_scale, z_in_scale,
    col_send, col_in, col_send_scale, col_in_scale,
    g_buf, g1, g2, g2_in, g3, g4, h_buf, h1, h2, h3, aug, solver,
    index_sem, prior_sem, tile_sem, gz_s, gz_r, gs_s, gs_r, gr_s, gr_r, sb_s, sb_r, zz_s, zz_r, zs_s, zs_r, cc_s, cc_r, cs_s, cs_r,
    red_row_s, red_row_r, red_col_s, red_col_r, al_row_s, al_row_r, al_col_s, al_col_r,
):
    Z = C // 2
    r, c = lax.axis_index("row"), lax.axis_index("col")
    z, core = c // 2, c % 2
    sib = z * 2 + (1 - core)
    pairs = [(b, a) for a in range(B) for b in range(a, B)]

    def local(s):
        return pltpu.make_async_copy(tiles_ref.at[s], tile_buf.at[s], tile_sem.at[s])

    def remote(src, dst, ssem, rsem, row, col):
        return pltpu.make_async_remote_copy(
            src_ref=src, dst_ref=dst, send_sem=ssem, recv_sem=rsem, device_id=(row, col), device_id_type=MESH
        )

    def loop(n, body):
        def step(k, carry):
            body(k)
            return carry

        lax.fori_loop(0, n, step, 0)

    index_copy = pltpu.make_async_copy(index_in, index_ref, index_sem)
    index_copy.start()
    prior_copies = [
        pltpu.make_async_copy(prior_ref.at[b], basis.at[pl.ds(b * K, K)], prior_sem.at[b]) for b in range(B - 1)
    ]
    for copy in prior_copies:
        copy.start()
    loop(S, lambda s: local(s).start())

    barrier = pltpu.get_barrier_semaphore()
    loop(C - 1, lambda k: pl.semaphore_signal(barrier, inc=1, device_id=(r, (c + 1 + k) % C), device_id_type=MESH))
    loop(R - 1, lambda k: pl.semaphore_signal(barrier, inc=1, device_id=((r + 1 + k) % R, c), device_id_type=MESH))
    pl.semaphore_wait(barrier, C + R - 2)

    def row_gather(k):
        peer = (r + 1 + k) % R
        return remote(probe_ref, colp.at[r], gr_s.at[peer], gr_r.at[r], peer, c)

    def z_gather(k):
        peer = (z + 1 + k) % Z
        return remote(probe_ref, rowp.at[c], gz_s.at[peer], gz_r.at[z], r, peer * 2 + core)

    def sib_gather(zz):
        slot = zz * 2 + core
        return remote(rowp.at[slot], rowp.at[slot], gs_s.at[zz], gs_r.at[zz], r, sib)

    def sib_arrival(zz):
        slot = zz * 2 + (1 - core)
        return remote(rowp.at[slot], rowp.at[slot], gs_s.at[zz], gs_r.at[zz], r, sib)

    loop(R - 1, lambda k: row_gather(k).start())
    loop(Z - 1, lambda k: z_gather(k).start())
    rowp[c] = probe_ref[...]
    colp[r] = probe_ref[...]
    sib_gather(z).start()

    def reducer(buf, in1, buf2, in2, all3, all4, rows):
        chunk = C * rows

        def p1(k):
            peer = (r + 1 + k) % R
            src = buf.at[pl.ds(pl.multiple_of(peer * chunk, 8), chunk)]
            return remote(src, in1.at[r], red_row_s.at[0, peer], red_row_r.at[0, r], peer, c)

        def p2(k):
            peer = (c + 1 + k) % C
            src = buf2.at[pl.ds(pl.multiple_of(peer * rows, 8), rows)]
            return remote(src, in2.at[c], red_col_s.at[0, peer], red_col_r.at[0, c], r, peer)

        def p3(k):
            peer = (c + 1 + k) % C
            return remote(all3.at[c], all3.at[c], red_col_s.at[1, peer], red_col_r.at[1, c], r, peer)

        def p4(k):
            peer = (r + 1 + k) % R
            return remote(all3, all4.at[r], red_row_s.at[1, peer], red_row_r.at[1, r], peer, c)

        def got_row(phase, dst, k):
            peer = (r + 1 + k) % R
            remote(dst.at[peer], dst.at[peer], red_row_s.at[phase, peer], red_row_r.at[phase, peer], peer, c).wait_recv()

        def got_col(phase, dst, k):
            peer = (c + 1 + k) % C
            remote(dst.at[peer], dst.at[peer], red_col_s.at[phase, peer], red_col_r.at[phase, peer], r, peer).wait_recv()

        def first():
            loop(R - 1, lambda k: p1(k).start())

        def second():
            buf2[...] = buf[pl.ds(pl.multiple_of(r * chunk, 8), chunk), :]

            def add(k):
                got_row(0, in1, k)
                buf2[...] += in1[(r + 1 + k) % R]

            loop(R - 1, add)
            loop(C - 1, lambda k: p2(k).start())

        def third():
            def add(k, total):
                got_col(0, in2, k)
                return total + in2[(c + 1 + k) % C]

            all3[c] = lax.fori_loop(0, C - 1, add, buf2[pl.ds(pl.multiple_of(c * rows, 8), rows), :])
            loop(C - 1, lambda k: p3(k).start())

        def fourth():
            loop(C - 1, lambda k: got_col(1, all3, k))
            loop(R - 1, lambda k: p4(k).start())
            all4[r] = all3[...]

        def fifth():
            loop(R - 1, lambda k: got_row(1, all4, k))

        def drain():
            loop(R - 1, lambda k: p1(k).wait_send())
            loop(C - 1, lambda k: p2(k).wait_send())
            loop(C - 1, lambda k: p3(k).wait_send())
            loop(R - 1, lambda k: p4(k).wait_send())

        return first, second, third, fourth, fifth, drain

    gram = reducer(g_buf, g1, g2, g2_in, g3, g4, g_rows)

    def a1(k):
        peer = (c + 1 + k) % C
        src = h_buf.at[pl.ds(pl.multiple_of(peer * h_rows, 8), h_rows)]
        return remote(src, h1.at[c], al_col_s.at[0, peer], al_col_r.at[0, c], r, peer)

    def a2(k):
        peer = (r + 1 + k) % R
        return remote(h2.at[r], h2.at[r], al_row_s.at[peer], al_row_r.at[r], peer, c)

    def a3(k):
        peer = (c + 1 + k) % C
        return remote(h3.at[c], h3.at[c], al_col_s.at[1, peer], al_col_r.at[1, c], r, peer)

    def got_a_col(phase, dst, k):
        peer = (c + 1 + k) % C
        remote(dst.at[peer], dst.at[peer], al_col_s.at[phase, peer], al_col_r.at[phase, peer], r, peer).wait_recv()

    def got_a_row(k):
        peer = (r + 1 + k) % R
        remote(h2.at[peer], h2.at[peer], al_row_s.at[peer], al_row_r.at[peer], peer, c).wait_recv()

    def along_parts():
        loop(C - 1, lambda k: a1(k).start())

    def along_sums():
        def add(k, total):
            got_a_col(0, h1, k)
            return total + h1[(c + 1 + k) % C]

        h2[r] = lax.fori_loop(0, C - 1, add, h_buf[pl.ds(pl.multiple_of(c * h_rows, 8), h_rows), :])
        loop(R - 1, lambda k: a2(k).start())

    def along_totals():
        loop(R - 1, got_a_row)
        h3[c] = lax.fori_loop(1, R, lambda k, total: total + h2[k], h2[0])
        loop(C - 1, lambda k: a3(k).start())

    def along_done():
        loop(C - 1, lambda k: got_a_col(1, h3, k))

    for copy in prior_copies:
        copy.wait()
    basis[(B - 1) * K :, :] = probe_ref[...]
    half = K // 2
    used = len(pairs) * half
    spot = 0
    for a in range(B):
        one = basis[a * K : (a + 1) * K, :]
        both = jnp.concatenate([one, one], axis=0)
        blocks = lax.dot_general(basis[a * K :, :], both, NT, preferred_element_type=F32)
        for b in range(a, B):
            g_buf[spot : spot + half, :] = pack(blocks[(b - a) * K : (b - a + 1) * K])
            spot += half
    if g_buf.shape[0] > used:
        g_buf[used:, :] = jnp.zeros((g_buf.shape[0] - used, 2 * K), F32)
    if h_buf.shape[0] > B * half:
        h_buf[B * half :, :] = jnp.zeros((h_buf.shape[0] - B * half, 2 * K), F32)
    gram[0]()

    def got_row_probe(k):
        peer = (r + 1 + k) % R
        remote(colp.at[peer], colp.at[peer], gr_s.at[peer], gr_r.at[peer], peer, c).wait_recv()

    loop(R - 1, got_row_probe)
    index_copy.wait()

    def forward(s):
        local(s).wait()
        right = colp[index_ref[1, s] // C]
        fwd[s] = lax.dot_general(tile_buf[s], right, NT, preferred_element_type=F32).T

    loop(S, forward)
    gram[1]()

    def pick(dst, parts, column, number, divide):
        hits = []
        for slot in range(S):
            value = index_ref[column, slot]
            place = value // C if divide else value % C
            hits.append(jnp.logical_and(place == number, index_ref[2, slot] > 0))

        def some(k):
            rows = pl.ds(pl.multiple_of(k * 16, 16), 16)
            total = jnp.where(hits[0], parts[0, rows, :], 0.0)
            for slot in range(1, S):
                total = total + jnp.where(hits[slot], parts[slot, rows, :], 0.0)
            dst[rows, :] = total

        loop(K // 16, some)

    def to_sib(zz):
        return remote(row_part.at[zz], sib_in.at[zz], sb_s.at[zz], sb_r.at[zz], r, sib)

    def give_sib(k):
        zz = (z + 1 + k) % Z
        pick(row_part.at[zz], fwd, 0, zz * 2 + (1 - core), False)
        to_sib(zz).start()

    loop(Z, give_sib)

    def share_probe(k):
        peer = (z + 1 + k) % Z
        slot = peer * 2 + core
        remote(rowp.at[slot], rowp.at[slot], gz_s.at[peer], gz_r.at[peer], r, slot).wait_recv()
        sib_gather(peer).start()

    loop(Z - 1, share_probe)
    gram[2]()

    def to_z(zz):
        return remote(z_send.at[zz], z_in.at[z], zz_s.at[zz], zz_r.at[z], r, zz * 2 + core)

    def to_z_scale(zz):
        return remote(z_send_scale.at[zz], z_in_scale.at[z], zs_s.at[zz], zs_r.at[z], r, zz * 2 + core)

    def chip_sum(zz):
        pick(z_sum, fwd, 0, zz * 2 + core, False)
        to_sib(zz).wait_recv()
        return z_sum[...] + sib_in[zz]

    def give_z(k):
        zz = (z + 1 + k) % Z
        z_send[zz], z_send_scale[zz] = code(chip_sum(zz))
        to_z(zz).start()
        to_z_scale(zz).start()

    loop(Z - 1, give_z)
    gram[3]()

    loop(Z, lambda zz: sib_arrival(zz).wait_recv())

    gram[4]()

    sums = g4[...].reshape(-1, 2 * K)
    gram_blocks = {}
    lanes = lane_of((K, 2 * K))
    down = lax.broadcasted_iota(jnp.int32, (K, 2 * K), 0)
    eye = jnp.where(lanes == down + K, 1.0, 0.0)
    for i, (b, a) in enumerate(pairs):
        packed = sums[i * half : (i + 1) * half]
        if a == b:
            whole = jnp.concatenate([packed, pltpu.roll(packed, K, 1)], axis=0)
            aug[b] = jnp.where(lanes < K, whole, eye)
        else:
            gram_blocks[b, a] = unpack(packed)

    all_lanes = lane_of((B, K, 2 * K))
    all_down = lax.broadcasted_iota(jnp.int32, (B, K, 2 * K), 1)
    row_lanes = lane_of((B, 1, 2 * K))

    def eliminate(k):
        one, two = 2 * k, 2 * k + 1
        whole = aug[...]
        row1, row2 = aug[:, pl.ds(one, 1), :], aug[:, pl.ds(two, 1), :]

        def at(values, where, number):
            return jnp.sum(jnp.where(where == number, values, 0.0), axis=2, keepdims=True)

        column1, column2 = at(whole, all_lanes, one), at(whole, all_lanes, two)
        p11, p12 = at(row1, row_lanes, one), at(row1, row_lanes, two)
        p21, p22 = at(row2, row_lanes, one), at(row2, row_lanes, two)
        first = 1.0 / p11
        ratio = p21 * first
        second = 1.0 / (p22 - p12 * ratio)
        scaled2 = (row2 - ratio * row1) * second
        scaled1 = (row1 - p12 * scaled2) * first
        rest = whole - column1 * scaled1 - column2 * scaled2
        aug[...] = jnp.where(all_down == one, scaled1, jnp.where(all_down == two, scaled2, rest))

    Q, wide = col_send.shape[1], col_send.shape[3]
    given = 1 if Q * (S + R - 1) <= K // 2 else 0
    per_chunk = S + given * (R - 1)

    def to_row(peer, q):
        return remote(col_send.at[peer, q], col_in.at[r, q], cc_s.at[peer, q], cc_r.at[r, q], peer, c)

    def to_row_scale(peer, q):
        return remote(
            col_send_scale.at[peer, q], col_in_scale.at[r, q], cs_s.at[peer, q], cs_r.at[r, q], peer, c
        )

    def chunk(q):
        columns = pl.ds(pl.multiple_of(q * wide, wide), wide)

        def mirror(s):
            left = rowp[index_ref[0, s] % C]
            mir[s, :, columns] = jnp.dot(left, tile_buf[s, :, columns], preferred_element_type=F32)
            eliminate(q * per_chunk + s)

        loop(S, mirror)

        def give_row(k):
            peer = (r + 1 + k) % R
            total = jnp.zeros((K, wide), F32)
            for slot in range(S):
                hit = jnp.logical_and(index_ref[1, slot] // C == peer, index_ref[2, slot] > 0)
                total = total + jnp.where(hit, mir[slot, :, columns], 0.0)
            col_send[peer, q], col_send_scale[peer, q] = code(total)
            to_row(peer, q).start()
            to_row_scale(peer, q).start()
            if given:
                eliminate(q * per_chunk + S + k)

        loop(R - 1, give_row)

    loop(Q, chunk)
    out_ref[...] = self_ref[...] * probe_ref[...].astype(F32) + chip_sum(z)
    pick(z_sum, mir, 1, r, True)
    out_ref[...] += z_sum[...]

    loop(K // 2 - Q * per_chunk, lambda k: eliminate(Q * per_chunk + k))

    inverse = [pltpu.roll(aug[b], K, 1)[:, :K] for b in range(B)]

    def solver_row(b):
        line = [inverse[b]]
        if b > 0:
            row = jnp.concatenate([gram_blocks[b, a] for a in range(b)], axis=1)
            scaled = jnp.dot(inverse[b], row, precision=HIGH, preferred_element_type=F32)
            done = solver[: b * K, : b * K]
            line = [-jnp.dot(scaled, done, precision=HIGH, preferred_element_type=F32), inverse[b]]
        if b < B - 1:
            line.append(jnp.zeros((K, (B - 1 - b) * K), F32))
        solver[b * K : (b + 1) * K, :] = jnp.concatenate(line, axis=1)

    solver_row(0)
    solver_row(1)

    def add_row(i):
        q, k = i // (R - 1), i % (R - 1)
        peer = (r + 1 + k) % R
        values, lines = col_in.at[peer, q], col_in_scale.at[peer, q]
        remote(values, values, cc_s.at[peer, q], cc_r.at[peer, q], peer, c).wait_recv()
        remote(lines, lines, cs_s.at[peer, q], cs_r.at[peer, q], peer, c).wait_recv()
        columns = pl.ds(pl.multiple_of(q * wide, wide), wide)
        out_ref[:, columns] += decode(col_in[peer, q], col_in_scale[peer, q])

    def add_z(k):
        peer = (z + 1 + k) % Z
        remote(z_in.at[peer], z_in.at[peer], zz_s.at[peer], zz_r.at[peer], r, peer * 2 + core).wait_recv()
        lines = z_in_scale.at[peer]
        remote(lines, lines, zs_s.at[peer], zs_r.at[peer], r, peer * 2 + core).wait_recv()
        out_ref[...] += decode(z_in[peer], z_in_scale[peer])

    loop(Z - 1, add_z)
    loop(Q * (R - 1), add_row)

    product = out_ref[...]
    hi, mid, lo = split3(product)
    parts = jnp.concatenate([lo, lo, mid, mid, hi, hi], axis=0)
    inner = lax.dot_general(basis[...], parts, NT, preferred_element_type=F32)
    inner = inner[:, : 2 * K] + inner[:, 2 * K : 4 * K] + inner[:, 4 * K :]
    for b in range(B):
        h_buf[b * half : (b + 1) * half, :] = pack(inner[b * K : (b + 1) * K])
    along_parts()
    for b in range(2, B - 2):
        solver_row(b)
    along_sums()
    solver_row(B - 2)
    along_totals()
    solver_row(B - 1)
    along_done()
    targets = h3[...].reshape(-1, 2 * K)
    stacked = jnp.concatenate([unpack(targets[b * half : (b + 1) * half]) for b in range(B)], axis=0)
    solved = jnp.dot(solver[...], stacked, precision=HIGH, preferred_element_type=F32)
    coef_ref[...] = solved.reshape(B, K, K)

    gram[5]()
    loop(C - 1, lambda k: a1(k).wait_send())
    loop(R - 1, lambda k: a2(k).wait_send())
    loop(C - 1, lambda k: a3(k).wait_send())
    loop(R - 1, lambda k: row_gather(k).wait_send())
    loop(Z - 1, lambda k: z_gather(k).wait_send())
    loop(Z, lambda zz: sib_gather(zz).wait_send())
    loop(Z, lambda zz: to_sib(zz).wait_send())
    loop(Z - 1, lambda k: to_z((z + 1 + k) % Z).wait_send())
    loop(Z - 1, lambda k: to_z_scale((z + 1 + k) % Z).wait_send())

    def row_left(i):
        q, k = i // (R - 1), i % (R - 1)
        to_row((r + 1 + k) % R, q).wait_send()
        to_row_scale((r + 1 + k) % R, q).wait_send()

    loop(Q * (R - 1), row_left)


def finish(product_ref, coef_ref, prior_ref, probe_ref, out_ref, coef_out):
    B, K, _ = coef_ref.shape
    coef_out[...] = coef_ref[...]
    stacked = coef_ref[...].reshape(B * K, K)
    last = (B - 1) * K
    parts = jnp.concatenate(split3(stacked.T)[::-1], axis=0)
    taken = jnp.dot(parts[:, :last], prior_ref[...].reshape(last, -1), preferred_element_type=F32)
    taken = taken + jnp.dot(parts[:, last:], probe_ref[...], preferred_element_type=F32)
    taken = taken[:K] + taken[K : 2 * K] + taken[2 * K :]
    out_ref[...] = product_ref[...] - taken


def shards(R, C, probe_block, prior_blocks, self_relatedness, tile_values, tile_index):
    K, T = probe_block.shape
    S = tile_values.shape[0]
    B = prior_blocks.shape[0] + 1
    Z = C // 2
    half = K // 2
    g_rows = round_up(-(-(B * (B + 1) // 2 * half) // (R * C)), 8)
    h_rows = round_up(-(-(B * half) // C), 8)
    vmem = lambda shape, dtype=F32: pltpu.VMEM(shape, dtype)
    dma = lambda *shape: pltpu.SemaphoreType.DMA(shape)
    W = 2 * K
    Q = T // 512

    def reduce_scratch(rows):
        return [
            vmem((R * C * rows, W)), vmem((R, C * rows, W)), vmem((C * rows, W)),
            vmem((C, rows, W)), vmem((C, rows, W)), vmem((R, C, rows, W)),
        ]

    scratch = [
        pltpu.SMEM(tile_index.shape[::-1], jnp.int32), vmem((S, T, T), BF16), vmem((B * K, T), BF16), vmem((C, K, T), BF16), vmem((R, K, T), BF16),
        vmem((S, K, T)), vmem((S, K, T)),
        vmem((Z, K, T)), vmem((Z, K, T)), vmem((K, T)),
        vmem((Z, K, T), I16), vmem((Z, K, T), I16), vmem((Z, 8, 128)), vmem((Z, 8, 128)),
        vmem((R, Q, K, T // Q), I16), vmem((R, Q, K, T // Q), I16), vmem((R, Q, 8, 128)), vmem((R, Q, 8, 128)),
        *reduce_scratch(g_rows),
        vmem((C * h_rows, W)), vmem((C, h_rows, W)), vmem((R, h_rows, W)), vmem((C, h_rows, W)),
        vmem((B, K, W)), vmem((B * K, B * K)),
        pltpu.SemaphoreType.DMA, dma(B - 1), dma(S), dma(Z), dma(Z), dma(Z), dma(Z), dma(R), dma(R), dma(Z), dma(Z),
        dma(Z), dma(Z), dma(Z), dma(Z), dma(R, Q), dma(R, Q), dma(R, Q), dma(R, Q),
        dma(2, R), dma(2, R), dma(2, C), dma(2, C), dma(R), dma(R), dma(2, C), dma(2, C),
    ]
    in_vmem = pl.BlockSpec(memory_space=pltpu.VMEM)
    in_any = pl.BlockSpec(memory_space=pl.ANY)
    product, coefficients = pl.pallas_call(
        functools.partial(kernel, R, C, S, B, K, g_rows, h_rows),
        out_shape=(jax.ShapeDtypeStruct((K, T), F32), jax.ShapeDtypeStruct((B, K, K), F32)),
        in_specs=[
            in_any, in_vmem, in_any, in_vmem, in_any,
        ],
        out_specs=(in_vmem, in_vmem),
        scratch_shapes=scratch,
        compiler_params=pltpu.CompilerParams(
            collective_id=0, has_side_effects=True, vmem_limit_bytes=56 * 1024 * 1024
        ),
        cost_estimate=pl.CostEstimate(
            flops=4 * S * K * T * T, bytes_accessed=2 * S * T * T, transcendentals=0
        ),
    )(tile_index.T, probe_block, prior_blocks, self_relatedness[None], tile_values)
    return pl.pallas_call(
        finish,
        out_shape=(jax.ShapeDtypeStruct((K, T), F32), jax.ShapeDtypeStruct((B, K, K), F32)),
        in_specs=[in_vmem] * 4,
        out_specs=(in_vmem, in_vmem),
    )(product, coefficients, prior_blocks, probe_block)


def solution(mesh):
    in_specs = (
        P(None, ("row", "col")),
        P(None, None, ("row", "col")),
        P(("row", "col")),
        P(("row", "col"), None, None),
        P(("row", "col"), None),
    )
    out_specs = (P(None, ("row", "col")), P())
    body = functools.partial(shards, mesh.shape["row"], mesh.shape["col"])
    return jax.shard_map(body, mesh=mesh, in_specs=in_specs, out_specs=out_specs, check_vma=False)
```

```python
import functools

import jax
import jax.numpy as jnp
from jax import lax
from jax.experimental import pallas as pl
from jax.experimental.pallas import tpu as pltpu
from jax.sharding import PartitionSpec as P

HIGH = lax.Precision.HIGHEST
MESH = pl.DeviceIdType.MESH
F32 = jnp.float32
BF16 = jnp.bfloat16
I16 = jnp.int16
NT = (((1,), (1,)), ((), ()))


def round_up(value, unit):
    return -(-value // unit) * unit


def split3(x):
    hi = x.astype(BF16)
    rest = x - hi.astype(F32)
    mid = rest.astype(BF16)
    lo = (rest - mid.astype(F32)).astype(BF16)
    return hi, mid, lo


def lane_of(shape):
    return lax.broadcasted_iota(jnp.int32, shape, len(shape) - 1)


def pack(block):
    half = block.shape[0] // 2
    return jnp.where(lane_of((half, block.shape[1])) < block.shape[1] // 2, block[:half], block[half:])


def unpack(packed):
    width = packed.shape[1] // 2
    return jnp.concatenate([packed[:, :width], pltpu.roll(packed, width, 1)[:, :width]], axis=0)


def code(block):
    rows = block.shape[0]
    most = jnp.maximum(jnp.max(jnp.abs(block), axis=1, keepdims=True), 1e-30)
    quantized = jnp.round(block * (32767.0 / most)).astype(jnp.int32).astype(jnp.int16)
    shape = (rows, 128)
    hit = lane_of(shape) == lax.broadcasted_iota(jnp.int32, shape, 0)
    line = jnp.sum(jnp.where(hit, most * (1.0 / 32767.0), 0.0), axis=0, keepdims=True)
    return quantized, jnp.broadcast_to(line, (8, 128))


def decode(quantized, lines):
    shape = (quantized.shape[0], 128)
    hit = lane_of(shape) == lax.broadcasted_iota(jnp.int32, shape, 0)
    scale = jnp.sum(jnp.where(hit, lines[:1], 0.0), axis=1, keepdims=True)
    return quantized.astype(jnp.int32).astype(F32) * scale


def kernel(
    R, C, S, B, K, g_rows, h_rows,
    index_in, probe_ref, prior_ref, self_ref, tiles_ref,
    out_ref, coef_ref,
    index_ref, tile_buf, basis, rowp, colp, fwd, mir, row_part, sib_in, z_sum, z_send, z_in, z_send_scale, z_in_scale,
    col_send, col_in, col_send_scale, col_in_scale,
    g_buf, g1, g2, g2_in, g3, g4, h_buf, h1, h2, h3, aug, solver,
    index_sem, prior_sem, tile_sem, gz_s, gz_r, gs_s, gs_r, gr_s, gr_r, sb_s, sb_r, zz_s, zz_r, zs_s, zs_r, cc_s, cc_r, cs_s, cs_r,
    red_row_s, red_row_r, red_col_s, red_col_r, al_row_s, al_row_r, al_col_s, al_col_r,
):
    Z = C // 2
    r, c = lax.axis_index("row"), lax.axis_index("col")
    z, core = c // 2, c % 2
    sib = z * 2 + (1 - core)
    pairs = [(b, a) for a in range(B) for b in range(a, B)]

    def local(s):
        return pltpu.make_async_copy(tiles_ref.at[s], tile_buf.at[s], tile_sem.at[s])

    def remote(src, dst, ssem, rsem, row, col):
        return pltpu.make_async_remote_copy(
            src_ref=src, dst_ref=dst, send_sem=ssem, recv_sem=rsem, device_id=(row, col), device_id_type=MESH
        )

    def loop(n, body):
        def step(k, carry):
            body(k)
            return carry

        lax.fori_loop(0, n, step, 0)

    index_copy = pltpu.make_async_copy(index_in, index_ref, index_sem)
    index_copy.start()
    prior_copies = [
        pltpu.make_async_copy(prior_ref.at[b], basis.at[pl.ds(b * K, K)], prior_sem.at[b]) for b in range(B - 1)
    ]
    for copy in prior_copies:
        copy.start()
    loop(S, lambda s: local(s).start())

    barrier = pltpu.get_barrier_semaphore()
    loop(C - 1, lambda k: pl.semaphore_signal(barrier, inc=1, device_id=(r, (c + 1 + k) % C), device_id_type=MESH))
    loop(R - 1, lambda k: pl.semaphore_signal(barrier, inc=1, device_id=((r + 1 + k) % R, c), device_id_type=MESH))
    pl.semaphore_wait(barrier, C + R - 2)

    def row_gather(k):
        peer = (r + 1 + k) % R
        return remote(probe_ref, colp.at[r], gr_s.at[peer], gr_r.at[r], peer, c)

    def z_gather(k):
        peer = (z + 1 + k) % Z
        return remote(probe_ref, rowp.at[c], gz_s.at[peer], gz_r.at[z], r, peer * 2 + core)

    def sib_gather(zz):
        slot = zz * 2 + core
        return remote(rowp.at[slot], rowp.at[slot], gs_s.at[zz], gs_r.at[zz], r, sib)

    def sib_arrival(zz):
        slot = zz * 2 + (1 - core)
        return remote(rowp.at[slot], rowp.at[slot], gs_s.at[zz], gs_r.at[zz], r, sib)

    loop(R - 1, lambda k: row_gather(k).start())
    loop(Z - 1, lambda k: z_gather(k).start())
    rowp[c] = probe_ref[...]
    colp[r] = probe_ref[...]
    sib_gather(z).start()

    def reducer(buf, in1, buf2, in2, all3, all4, rows):
        chunk = C * rows

        def p1(k):
            peer = (r + 1 + k) % R
            src = buf.at[pl.ds(pl.multiple_of(peer * chunk, 8), chunk)]
            return remote(src, in1.at[r], red_row_s.at[0, peer], red_row_r.at[0, r], peer, c)

        def p2(k):
            peer = (c + 1 + k) % C
            src = buf2.at[pl.ds(pl.multiple_of(peer * rows, 8), rows)]
            return remote(src, in2.at[c], red_col_s.at[0, peer], red_col_r.at[0, c], r, peer)

        def p3(k):
            peer = (c + 1 + k) % C
            return remote(all3.at[c], all3.at[c], red_col_s.at[1, peer], red_col_r.at[1, c], r, peer)

        def p4(k):
            peer = (r + 1 + k) % R
            return remote(all3, all4.at[r], red_row_s.at[1, peer], red_row_r.at[1, r], peer, c)

        def got_row(phase, dst, k):
            peer = (r + 1 + k) % R
            remote(dst.at[peer], dst.at[peer], red_row_s.at[phase, peer], red_row_r.at[phase, peer], peer, c).wait_recv()

        def got_col(phase, dst, k):
            peer = (c + 1 + k) % C
            remote(dst.at[peer], dst.at[peer], red_col_s.at[phase, peer], red_col_r.at[phase, peer], r, peer).wait_recv()

        def first():
            loop(R - 1, lambda k: p1(k).start())

        def second():
            buf2[...] = buf[pl.ds(pl.multiple_of(r * chunk, 8), chunk), :]

            def add(k):
                got_row(0, in1, k)
                buf2[...] += in1[(r + 1 + k) % R]

            loop(R - 1, add)
            loop(C - 1, lambda k: p2(k).start())

        def third():
            def add(k, total):
                got_col(0, in2, k)
                return total + in2[(c + 1 + k) % C]

            all3[c] = lax.fori_loop(0, C - 1, add, buf2[pl.ds(pl.multiple_of(c * rows, 8), rows), :])
            loop(C - 1, lambda k: p3(k).start())

        def fourth():
            loop(C - 1, lambda k: got_col(1, all3, k))
            loop(R - 1, lambda k: p4(k).start())
            all4[r] = all3[...]

        def fifth():
            loop(R - 1, lambda k: got_row(1, all4, k))

        def drain():
            loop(R - 1, lambda k: p1(k).wait_send())
            loop(C - 1, lambda k: p2(k).wait_send())
            loop(C - 1, lambda k: p3(k).wait_send())
            loop(R - 1, lambda k: p4(k).wait_send())

        return first, second, third, fourth, fifth, drain

    gram = reducer(g_buf, g1, g2, g2_in, g3, g4, g_rows)

    def a1(k):
        peer = (c + 1 + k) % C
        src = h_buf.at[pl.ds(pl.multiple_of(peer * h_rows, 8), h_rows)]
        return remote(src, h1.at[c], al_col_s.at[0, peer], al_col_r.at[0, c], r, peer)

    def a2(k):
        peer = (r + 1 + k) % R
        return remote(h2.at[r], h2.at[r], al_row_s.at[peer], al_row_r.at[r], peer, c)

    def a3(k):
        peer = (c + 1 + k) % C
        return remote(h3.at[c], h3.at[c], al_col_s.at[1, peer], al_col_r.at[1, c], r, peer)

    def got_a_col(phase, dst, k):
        peer = (c + 1 + k) % C
        remote(dst.at[peer], dst.at[peer], al_col_s.at[phase, peer], al_col_r.at[phase, peer], r, peer).wait_recv()

    def got_a_row(k):
        peer = (r + 1 + k) % R
        remote(h2.at[peer], h2.at[peer], al_row_s.at[peer], al_row_r.at[peer], peer, c).wait_recv()

    def along_parts():
        loop(C - 1, lambda k: a1(k).start())

    def along_sums():
        def add(k, total):
            got_a_col(0, h1, k)
            return total + h1[(c + 1 + k) % C]

        h2[r] = lax.fori_loop(0, C - 1, add, h_buf[pl.ds(pl.multiple_of(c * h_rows, 8), h_rows), :])
        loop(R - 1, lambda k: a2(k).start())

    def along_totals():
        loop(R - 1, got_a_row)
        h3[c] = lax.fori_loop(1, R, lambda k, total: total + h2[k], h2[0])
        loop(C - 1, lambda k: a3(k).start())

    def along_done():
        loop(C - 1, lambda k: got_a_col(1, h3, k))

    for copy in prior_copies:
        copy.wait()
    basis[(B - 1) * K :, :] = probe_ref[...]
    half = K // 2
    used = len(pairs) * half
    spot = 0
    for a in range(B):
        one = basis[a * K : (a + 1) * K, :]
        both = jnp.concatenate([one, one], axis=0)
        blocks = lax.dot_general(basis[a * K :, :], both, NT, preferred_element_type=F32)
        for b in range(a, B):
            g_buf[spot : spot + half, :] = pack(blocks[(b - a) * K : (b - a + 1) * K])
            spot += half
    if g_buf.shape[0] > used:
        g_buf[used:, :] = jnp.zeros((g_buf.shape[0] - used, 2 * K), F32)
    if h_buf.shape[0] > B * half:
        h_buf[B * half :, :] = jnp.zeros((h_buf.shape[0] - B * half, 2 * K), F32)
    gram[0]()

    def got_row_probe(k):
        peer = (r + 1 + k) % R
        remote(colp.at[peer], colp.at[peer], gr_s.at[peer], gr_r.at[peer], peer, c).wait_recv()

    loop(R - 1, got_row_probe)
    index_copy.wait()

    def forward(s):
        local(s).wait()
        right = colp[index_ref[1, s] // C]
        fwd[s] = lax.dot_general(tile_buf[s], right, NT, preferred_element_type=F32).T

    loop(S, forward)
    gram[1]()

    def pick(dst, parts, column, number, divide):
        hits = []
        for slot in range(S):
            value = index_ref[column, slot]
            place = value // C if divide else value % C
            hits.append(jnp.logical_and(place == number, index_ref[2, slot] > 0))

        def some(k):
            rows = pl.ds(pl.multiple_of(k * 16, 16), 16)
            total = jnp.where(hits[0], parts[0, rows, :], 0.0)
            for slot in range(1, S):
                total = total + jnp.where(hits[slot], parts[slot, rows, :], 0.0)
            dst[rows, :] = total

        loop(K // 16, some)

    def to_sib(zz):
        return remote(row_part.at[zz], sib_in.at[zz], sb_s.at[zz], sb_r.at[zz], r, sib)

    def give_sib(k):
        zz = (z + 1 + k) % Z
        pick(row_part.at[zz], fwd, 0, zz * 2 + (1 - core), False)
        to_sib(zz).start()

    loop(Z, give_sib)

    def share_probe(k):
        peer = (z + 1 + k) % Z
        slot = peer * 2 + core
        remote(rowp.at[slot], rowp.at[slot], gz_s.at[peer], gz_r.at[peer], r, slot).wait_recv()
        sib_gather(peer).start()

    loop(Z - 1, share_probe)
    gram[2]()

    def to_z(zz):
        return remote(z_send.at[zz], z_in.at[z], zz_s.at[zz], zz_r.at[z], r, zz * 2 + core)

    def to_z_scale(zz):
        return remote(z_send_scale.at[zz], z_in_scale.at[z], zs_s.at[zz], zs_r.at[z], r, zz * 2 + core)

    def chip_sum(zz):
        pick(z_sum, fwd, 0, zz * 2 + core, False)
        to_sib(zz).wait_recv()
        return z_sum[...] + sib_in[zz]

    def give_z(k):
        zz = (z + 1 + k) % Z
        z_send[zz], z_send_scale[zz] = code(chip_sum(zz))
        to_z(zz).start()
        to_z_scale(zz).start()

    loop(Z - 1, give_z)
    gram[3]()

    loop(Z, lambda zz: sib_arrival(zz).wait_recv())

    Q, wide = col_send.shape[1], col_send.shape[3]
    per_body = K // 2 // (2 * S)
    given = 2 if 2 * (R - 1) + per_body * S <= K // 2 else 0
    shared = per_body * S + given * (R - 1)

    def to_row(peer, q):
        return remote(col_send.at[peer, q], col_in.at[r, q], cc_s.at[peer, q], cc_r.at[r, q], peer, c)

    def to_row_scale(peer, q):
        return remote(
            col_send_scale.at[peer, q], col_in_scale.at[r, q], cs_s.at[peer, q], cs_r.at[r, q], peer, c
        )

    def chunk(q, step=None):
        columns = pl.ds(q * wide, wide)

        def mirror(s):
            left = rowp[index_ref[0, s] % C]
            mir[s, :, columns] = jnp.dot(left, tile_buf[s, :, columns], preferred_element_type=F32)
            if step is not None:
                for i in range(per_body):
                    step(per_body * s + i)

        loop(S, mirror)

        def give_row(k):
            peer = (r + 1 + k) % R
            total = jnp.zeros((K, wide), F32)
            for slot in range(S):
                hit = jnp.logical_and(index_ref[1, slot] // C == peer, index_ref[2, slot] > 0)
                total = total + jnp.where(hit, mir[slot, :, columns], 0.0)
            col_send[peer, q], col_send_scale[peer, q] = code(total)
            to_row(peer, q).start()
            to_row_scale(peer, q).start()
            if step is not None:
                for i in range(given):
                    step(per_body * S + given * k + i)

        loop(R - 1, give_row)

    for q in range(Q - 1):
        chunk(q)
    gram[4]()

    sums = g4[...].reshape(-1, 2 * K)
    gram_blocks = {}
    lanes = lane_of((K, 2 * K))
    down = lax.broadcasted_iota(jnp.int32, (K, 2 * K), 0)
    eye = jnp.where(lanes == down + K, 1.0, 0.0)
    for i, (b, a) in enumerate(pairs):
        packed = sums[i * half : (i + 1) * half]
        if a == b:
            whole = jnp.concatenate([packed, pltpu.roll(packed, K, 1)], axis=0)
            aug[b] = jnp.where(lanes < K, whole, eye)
        else:
            gram_blocks[b, a] = unpack(packed)

    all_lanes = lane_of((B, K, 2 * K))
    all_down = lax.broadcasted_iota(jnp.int32, (B, K, 2 * K), 1)
    row_lanes = lane_of((B, 1, 2 * K))

    def eliminate(k):
        one, two = 2 * k, 2 * k + 1
        whole = aug[...]
        row1, row2 = aug[:, pl.ds(one, 1), :], aug[:, pl.ds(two, 1), :]

        def at(values, where, number):
            return jnp.sum(jnp.where(where == number, values, 0.0), axis=2, keepdims=True)

        column1, column2 = at(whole, all_lanes, one), at(whole, all_lanes, two)
        p11, p12 = at(row1, row_lanes, one), at(row1, row_lanes, two)
        p21, p22 = at(row2, row_lanes, one), at(row2, row_lanes, two)
        first = 1.0 / p11
        ratio = p21 * first
        second = 1.0 / (p22 - p12 * ratio)
        scaled2 = (row2 - ratio * row1) * second
        scaled1 = (row1 - p12 * scaled2) * first
        rest = whole - column1 * scaled1 - column2 * scaled2
        aug[...] = jnp.where(all_down == one, scaled1, jnp.where(all_down == two, scaled2, rest))

    chunk(Q - 1, eliminate)
    out_ref[...] = self_ref[...] * probe_ref[...].astype(F32) + chip_sum(z)
    pick(z_sum, mir, 1, r, True)
    out_ref[...] += z_sum[...]

    loop(K // 2 - shared, lambda k: eliminate(shared + k))

    inverse = [pltpu.roll(aug[b], K, 1)[:, :K] for b in range(B)]

    def solver_row(b):
        line = [inverse[b]]
        if b > 0:
            row = jnp.concatenate([gram_blocks[b, a] for a in range(b)], axis=1)
            scaled = jnp.dot(inverse[b], row, precision=HIGH, preferred_element_type=F32)
            done = solver[: b * K, : b * K]
            line = [-jnp.dot(scaled, done, precision=HIGH, preferred_element_type=F32), inverse[b]]
        if b < B - 1:
            line.append(jnp.zeros((K, (B - 1 - b) * K), F32))
        solver[b * K : (b + 1) * K, :] = jnp.concatenate(line, axis=1)

    solver_row(0)
    solver_row(1)

    def add_row(i):
        q, k = i // (R - 1), i % (R - 1)
        peer = (r + 1 + k) % R
        values, lines = col_in.at[peer, q], col_in_scale.at[peer, q]
        remote(values, values, cc_s.at[peer, q], cc_r.at[peer, q], peer, c).wait_recv()
        remote(lines, lines, cs_s.at[peer, q], cs_r.at[peer, q], peer, c).wait_recv()
        columns = pl.ds(pl.multiple_of(q * wide, wide), wide)
        out_ref[:, columns] += decode(col_in[peer, q], col_in_scale[peer, q])

    def add_z(k):
        peer = (z + 1 + k) % Z
        remote(z_in.at[peer], z_in.at[peer], zz_s.at[peer], zz_r.at[peer], r, peer * 2 + core).wait_recv()
        lines = z_in_scale.at[peer]
        remote(lines, lines, zs_s.at[peer], zs_r.at[peer], r, peer * 2 + core).wait_recv()
        out_ref[...] += decode(z_in[peer], z_in_scale[peer])

    loop(Z - 1, add_z)
    loop(Q * (R - 1), add_row)

    product = out_ref[...]
    hi, mid, lo = split3(product)
    parts = jnp.concatenate([lo, lo, mid, mid, hi, hi], axis=0)
    inner = lax.dot_general(basis[...], parts, NT, preferred_element_type=F32)
    inner = inner[:, : 2 * K] + inner[:, 2 * K : 4 * K] + inner[:, 4 * K :]
    for b in range(B):
        h_buf[b * half : (b + 1) * half, :] = pack(inner[b * K : (b + 1) * K])
    along_parts()
    for b in range(2, B - 2):
        solver_row(b)
    along_sums()
    solver_row(B - 2)
    along_totals()
    solver_row(B - 1)
    along_done()
    targets = h3[...].reshape(-1, 2 * K)
    stacked = jnp.concatenate([unpack(targets[b * half : (b + 1) * half]) for b in range(B)], axis=0)
    solved = jnp.dot(solver[...], stacked, precision=HIGH, preferred_element_type=F32)
    coef_ref[...] = solved.reshape(B, K, K)

    gram[5]()
    loop(C - 1, lambda k: a1(k).wait_send())
    loop(R - 1, lambda k: a2(k).wait_send())
    loop(C - 1, lambda k: a3(k).wait_send())
    loop(R - 1, lambda k: row_gather(k).wait_send())
    loop(Z - 1, lambda k: z_gather(k).wait_send())
    loop(Z, lambda zz: sib_gather(zz).wait_send())
    loop(Z, lambda zz: to_sib(zz).wait_send())
    loop(Z - 1, lambda k: to_z((z + 1 + k) % Z).wait_send())
    loop(Z - 1, lambda k: to_z_scale((z + 1 + k) % Z).wait_send())

    def row_left(i):
        q, k = i // (R - 1), i % (R - 1)
        to_row((r + 1 + k) % R, q).wait_send()
        to_row_scale((r + 1 + k) % R, q).wait_send()

    loop(Q * (R - 1), row_left)


def finish(product_ref, coef_ref, prior_ref, probe_ref, out_ref, coef_out):
    B, K, _ = coef_ref.shape
    coef_out[...] = coef_ref[...]
    stacked = coef_ref[...].reshape(B * K, K)
    last = (B - 1) * K
    parts = jnp.concatenate(split3(stacked.T)[::-1], axis=0)
    taken = jnp.dot(parts[:, :last], prior_ref[...].reshape(last, -1), preferred_element_type=F32)
    taken = taken + jnp.dot(parts[:, last:], probe_ref[...], preferred_element_type=F32)
    taken = taken[:K] + taken[K : 2 * K] + taken[2 * K :]
    out_ref[...] = product_ref[...] - taken


def shards(R, C, probe_block, prior_blocks, self_relatedness, tile_values, tile_index):
    K, T = probe_block.shape
    S = tile_values.shape[0]
    B = prior_blocks.shape[0] + 1
    Z = C // 2
    half = K // 2
    g_rows = round_up(-(-(B * (B + 1) // 2 * half) // (R * C)), 8)
    h_rows = round_up(-(-(B * half) // C), 8)
    vmem = lambda shape, dtype=F32: pltpu.VMEM(shape, dtype)
    dma = lambda *shape: pltpu.SemaphoreType.DMA(shape)
    W = 2 * K
    Q = T // 512

    def reduce_scratch(rows):
        return [
            vmem((R * C * rows, W)), vmem((R, C * rows, W)), vmem((C * rows, W)),
            vmem((C, rows, W)), vmem((C, rows, W)), vmem((R, C, rows, W)),
        ]

    scratch = [
        pltpu.SMEM(tile_index.shape[::-1], jnp.int32), vmem((S, T, T), BF16), vmem((B * K, T), BF16), vmem((C, K, T), BF16), vmem((R, K, T), BF16),
        vmem((S, K, T)), vmem((S, K, T)),
        vmem((Z, K, T)), vmem((Z, K, T)), vmem((K, T)),
        vmem((Z, K, T), I16), vmem((Z, K, T), I16), vmem((Z, 8, 128)), vmem((Z, 8, 128)),
        vmem((R, Q, K, T // Q), I16), vmem((R, Q, K, T // Q), I16), vmem((R, Q, 8, 128)), vmem((R, Q, 8, 128)),
        *reduce_scratch(g_rows),
        vmem((C * h_rows, W)), vmem((C, h_rows, W)), vmem((R, h_rows, W)), vmem((C, h_rows, W)),
        vmem((B, K, W)), vmem((B * K, B * K)),
        pltpu.SemaphoreType.DMA, dma(B - 1), dma(S), dma(Z), dma(Z), dma(Z), dma(Z), dma(R), dma(R), dma(Z), dma(Z),
        dma(Z), dma(Z), dma(Z), dma(Z), dma(R, Q), dma(R, Q), dma(R, Q), dma(R, Q),
        dma(2, R), dma(2, R), dma(2, C), dma(2, C), dma(R), dma(R), dma(2, C), dma(2, C),
    ]
    in_vmem = pl.BlockSpec(memory_space=pltpu.VMEM)
    in_any = pl.BlockSpec(memory_space=pl.ANY)
    product, coefficients = pl.pallas_call(
        functools.partial(kernel, R, C, S, B, K, g_rows, h_rows),
        out_shape=(jax.ShapeDtypeStruct((K, T), F32), jax.ShapeDtypeStruct((B, K, K), F32)),
        in_specs=[
            in_any, in_vmem, in_any, in_vmem, in_any,
        ],
        out_specs=(in_vmem, in_vmem),
        scratch_shapes=scratch,
        compiler_params=pltpu.CompilerParams(
            collective_id=0, has_side_effects=True, vmem_limit_bytes=56 * 1024 * 1024
        ),
        cost_estimate=pl.CostEstimate(
            flops=4 * S * K * T * T, bytes_accessed=2 * S * T * T, transcendentals=0
        ),
    )(tile_index.T, probe_block, prior_blocks, self_relatedness[None], tile_values)
    return pl.pallas_call(
        finish,
        out_shape=(jax.ShapeDtypeStruct((K, T), F32), jax.ShapeDtypeStruct((B, K, K), F32)),
        in_specs=[in_vmem] * 4,
        out_specs=(in_vmem, in_vmem),
    )(product, coefficients, prior_blocks, probe_block)


def solution(mesh):
    in_specs = (
        P(None, ("row", "col")),
        P(None, None, ("row", "col")),
        P(("row", "col")),
        P(("row", "col"), None, None),
        P(("row", "col"), None),
    )
    out_specs = (P(None, ("row", "col")), P())
    body = functools.partial(shards, mesh.shape["row"], mesh.shape["col"])
    return jax.shard_map(body, mesh=mesh, in_specs=in_specs, out_specs=out_specs, check_vma=False)
```
